512 devices in a mesh: pts: 512 (over z, y, x, core).
Axes of the slice: x: 4, y: 4, z: 16, core: 2. Of those that a mesh axis runs over, the one named last changes fastest.
Arguments:
- right_side: float32 [128, 524288], P(None, 'pts')
- coordinates: float32 [3, 524288], P(None, 'pts'), may hold values from -1 to 1
- tree_order: int32 [512, 1024], P('pts'), may hold values from 0 to 1023, each once within a row
- leaf_sizes: int32 [512, 2], P('pts'), may hold values from 1 to 640, 1024 in all within a row
- level_basis: bfloat16 [10, 32, 524288], P(None, None, 'pts'), may hold values from -6 to 6
- coupling: float32 [512, 10, 64, 64], P('pts'), as said below
Outputs:
- solution: float32 [128, 524288], P(None, 'pts')
- residual: float32 [128, 524288], P(None, 'pts')
The draws below stay inside these ranges and needn't reach their ends.
Inputs may be any that keep to these rules, and one draw needn't show every extreme that they name: `tree_order`: each row is a permutation of 0 to 1023. `leaf_sizes`: each device's two leaf sizes sum to 1024; each leaf holds at least 384 points. `coupling`: at level 0 the first 32 rows of a device's factor belong to its first leaf and the rest to its second; at a level l of 1 or more all devices whose indices agree from bit l up hold one factor, its first 32 rows belonging to the node whose bit l - 1 is 0, and devices whose bit l - 1 is 1 hold it with the two halves of rows exchanged.
All inputs are finite; a program needn't handle non-finite values.
Results may differ from the reference program's by a relative error of at most 0.007.
Values sent between devices are 32-bit elements; how exact they have to be, the bound alone decides.
No kernel may reach another device: no remote copies, remote signals or barrier semaphores. Data moves between devices by JAX's collectives and lax.ppermute only.
A program may use at most 64 MiB of HBM per device.

```python
import math
import jax
import jax.numpy as jnp
import numpy as np
from jax import lax

PTS_DEV = 1024
R = 32
NRHS = 128
ITERS = 2
LEAF_MOST = 640
LEVELS = 10
POINTS = 524288
N_PTS = 512


def draw_right_side(key, part):
    key = jax.random.fold_in(key, 11)
    count = PTS_DEV * N_PTS
    draw_shape = (NRHS, count)
    position = jnp.arange(count, dtype=jnp.float32) / (count - 1)
    base_draw = jax.random.truncated_normal(key, -4.0, 4.0, draw_shape, jnp.float32)
    rise_factor = 3.0 ** (0.5 * position)
    return base_draw * rise_factor[None, :]


def draw_coupling(key, part):
    key = jax.random.fold_in(key, 23)
    devices = jnp.arange(N_PTS, dtype=jnp.int32)
    levels = jnp.arange(LEVELS, dtype=jnp.int32)

    def one_block(device, level_idx):
        pair_index = jnp.right_shift(device, level_idx)
        side_bit = jnp.where(level_idx > 0, jnp.right_shift(device, jnp.maximum(level_idx - 1, 0)) % 2, 0)
        factor = jax.random.truncated_normal(jax.random.fold_in(jax.random.fold_in(key, level_idx), pair_index), -4.0, 4.0, (2 * R, 2 * R), jnp.float32)
        node_points = jnp.where(level_idx > 0, PTS_DEV * 2.0 ** (level_idx - 1), PTS_DEV / 2.0)
        factor = factor * 0.054 * node_points ** (-0.25)
        swapped = jnp.concatenate([factor[R:], factor[:R]], axis=0)
        return jnp.where(side_bit == 1, swapped, factor)
    return jax.vmap(jax.vmap(one_block, (None, 0)), (0, None))(devices, levels)


def steps_of(stream_key, extent, pieces, least, high):
    gain, own = 1.0, jax.random.fold_in(stream_key, 6)
    for dim, blocks in pieces:
        steps = jnp.exp(jax.random.uniform(jax.random.fold_in(own, dim), (blocks,), jnp.float32, least / len(pieces), high / len(pieces)))
        gain = gain * jnp.repeat(steps, extent[dim] // blocks).reshape([-1 if axis == dim else 1 for axis in range(len(extent))])
    return gain


def length_profile(number_of, total, reach, skew):
    weights = [(1 << 20) // math.isqrt(grade ** skew) + 1 for grade in range(2, number_of + 1)]
    surplus, holding = total - reach - (number_of - 1), [1] * (number_of - 1)
    while surplus > 0:
        movable = [i for i in range(number_of - 1) if holding[i] < reach]
        mass, remaining = sum([weights[i] for i in movable]), surplus
        for i in movable:
            addition = min(reach - holding[i], max(1, remaining * weights[i] // mass), surplus)
            holding[i] = holding[i] + addition
            surplus = surplus - addition
    return np.array([reach] + holding)


def ragged(stream_key, count, total, limit, slope):
    if count == 2:
        one = jax.random.randint(stream_key, (), max(1, total - limit), min(limit, total - 1) + 1)
        return jnp.stack([one, total - one])
    sizes = jnp.asarray(length_profile(count, total, limit, slope), jnp.int32)
    couples = (count - 1) // 2
    donor, sink = sizes[1:1 + 2 * couples:2], sizes[2:2 + 2 * couples:2]
    margin = jnp.minimum(donor - 1, limit - sink)
    shifted = jax.random.randint(jax.random.fold_in(stream_key, 1), (couples,), 0, 1 << 20) % (margin + 1)
    sizes = sizes.at[1:1 + 2 * couples:2].set(donor - shifted).at[2:2 + 2 * couples:2].set(sink + shifted)
    return sizes[jax.random.permutation(jax.random.fold_in(stream_key, 2), count)]


def normal_values(stream_key, dims, scale, most, shards=(), kind=jnp.bfloat16):
    drawn = jax.random.normal(stream_key, dims, jnp.float32) * scale
    if len(shards) > 0:
        drawn = steps_of(stream_key, dims, shards, -0.22, 0.18) * drawn
    return jnp.clip(drawn, min=-most, max=most).astype(kind)


def setup_inputs(seed: int = 0) -> dict:
    splits = jax.random.split(jax.random.key(seed), 7)
    right_side = draw_right_side(jax.random.fold_in(splits[6], 71), 0)
    coordinates = jnp.clip(jax.random.uniform(splits[1], (3, POINTS), jnp.float32, -1.0, 1.0) * steps_of(splits[1], (3, POINTS), ((1, 512),), -0.4, 0.0), -1.0, 1.0)
    tree_order = jax.vmap(lambda own: jax.random.permutation(own, PTS_DEV))(jax.random.split(splits[2], N_PTS)).reshape((N_PTS, PTS_DEV)).astype(jnp.int32)
    leaf_sizes = jax.vmap(lambda own: ragged(own, 2, PTS_DEV, LEAF_MOST, 0))(jax.random.split(splits[3], N_PTS)).reshape((N_PTS, 2)).astype(jnp.int32)
    level_basis = normal_values(splits[4], (LEVELS, R, POINTS), 1.0, 6.0, ((2, 512),))
    coupling = draw_coupling(jax.random.fold_in(splits[6], 71), 0)
    return {"right_side": right_side, "coordinates": coordinates, "tree_order": tree_order, "leaf_sizes": leaf_sizes, "level_basis": level_basis, "coupling": coupling}


SQRT_THREE = 1.7320508075688772
NOISE_VAR = 1.0

def kernel_columns(points, boundary, col_start, column_width):
    row_count = points.shape[1]
    columns = lax.dynamic_slice_in_dim(points, col_start, column_width, 1)
    dist_sq = jnp.zeros((row_count, column_width), jnp.float32)
    for component in range(3):
        offset = points[component][:, None] - columns[component][None, :]
        dist_sq = dist_sq + offset * offset
    scaled = SQRT_THREE * jnp.sqrt(dist_sq)
    values = (1.0 + scaled) * jnp.exp(-scaled)
    row_ids = lax.iota(jnp.int32, row_count)
    col_ids = col_start + lax.iota(jnp.int32, column_width)
    same_leaf = (row_ids < boundary)[:, None] == (col_ids < boundary)[None, :]
    values = jnp.where(same_leaf, values, 0.0) + jnp.where(row_ids[:, None] == col_ids[None, :], NOISE_VAR, 0.0)
    return values.astype(jnp.bfloat16)

def reference(right_side, coordinates, tree_order, leaf_sizes, level_basis, coupling):
    highest = lax.Precision.HIGHEST
    points_all = coordinates.reshape(3, N_PTS, PTS_DEV)
    ordered = jnp.take_along_axis(points_all, tree_order[None, :, :], axis=2)
    boundary_all = leaf_sizes[:, 0]
    own_half = coupling[:, :, :R, :]
    sib_half = coupling[:, :, R:, :]
    self_block = jnp.einsum('dlrc,dlsc->dlrs', own_half, own_half, precision=highest)
    cross_block = jnp.einsum('dlrc,dlsc->dlrs', own_half, sib_half, precision=highest)
    second_block = jnp.einsum('drc,dsc->drs', sib_half[:, 0], sib_half[:, 0], precision=highest)
    device_ids = jnp.arange(N_PTS, dtype=jnp.int32)

    def device_basis(device):
        return lax.dynamic_slice_in_dim(level_basis, device * PTS_DEV, PTS_DEV, 2).astype(jnp.float32)

    def apply(rounded):

        def first_pass(device):
            points = ordered[:, device]
            boundary = boundary_all[device]
            basis_dev = device_basis(device)
            probe_block = lax.dynamic_slice_in_dim(rounded, device * PTS_DEV, PTS_DEV, 1)
            kernel_tile = kernel_columns(points, boundary, 0, PTS_DEV)
            leaf_term = jnp.dot(probe_block, kernel_tile, preferred_element_type=jnp.float32)
            probe_wide = probe_block.astype(jnp.float32)
            projected = jnp.einsum('lrp,kp->lrk', basis_dev[1:], probe_wide)
            first_leaf = lax.iota(jnp.int32, PTS_DEV) < boundary
            proj_first = jnp.einsum('rp,kp->rk', basis_dev[0], jnp.where(first_leaf[None, :], probe_wide, 0.0))
            proj_second = jnp.einsum('rp,kp->rk', basis_dev[0], jnp.where(first_leaf[None, :], 0.0, probe_wide))
            return (leaf_term, projected, proj_first, proj_second)
        leaf_terms, projected, proj_first, proj_second = lax.map(first_pass, device_ids)
        coefficient_list = []
        for level_idx in range(1, LEVELS):
            group_size = 2 ** (level_idx - 1)
            node_sums = projected[:, level_idx - 1].reshape(N_PTS // group_size, group_size, R, NRHS).sum(axis=1)
            sibling = node_sums.reshape(-1, 2, R, NRHS)[:, ::-1].reshape(N_PTS // group_size, R, NRHS)
            own_full = jnp.repeat(node_sums, group_size, axis=0)
            sib_full = jnp.repeat(sibling, group_size, axis=0)
            combined = jnp.einsum('drs,dsk->drk', self_block[:, level_idx], own_full, precision=highest)
            combined = combined + jnp.einsum('drs,dsk->drk', cross_block[:, level_idx], sib_full, precision=highest)
            coefficient_list.append(combined.astype(jnp.bfloat16))
        coefficients = jnp.stack(coefficient_list, axis=1)
        coef_first = (jnp.einsum('drs,dsk->drk', self_block[:, 0], proj_first, precision=highest) + jnp.einsum('drs,dsk->drk', cross_block[:, 0], proj_second, precision=highest)).astype(jnp.bfloat16)
        coef_second = (jnp.einsum('drs,dsk->drk', second_block, proj_second, precision=highest) + jnp.einsum('dsr,dsk->drk', cross_block[:, 0], proj_first, precision=highest)).astype(jnp.bfloat16)

        def second_pass(device):
            basis_dev = device_basis(device)
            expanded = jnp.einsum('lrk,lrp->kp', coefficients[device].astype(jnp.float32), basis_dev[1:])
            first_leaf = lax.iota(jnp.int32, PTS_DEV) < boundary_all[device]
            local_first = jnp.einsum('rk,rp->kp', coef_first[device].astype(jnp.float32), basis_dev[0])
            local_second = jnp.einsum('rk,rp->kp', coef_second[device].astype(jnp.float32), basis_dev[0])
            local_term = jnp.where(first_leaf[None, :], local_first, local_second)
            return leaf_terms[device] + expanded + local_term
        blocks = lax.map(second_pass, device_ids)
        return jnp.transpose(blocks, (1, 0, 2)).reshape(NRHS, N_PTS * PTS_DEV)
    solution = jnp.zeros_like(right_side)
    residual = right_side
    direction = right_side
    norm_now = lax.optimization_barrier(jnp.sum(residual * residual, axis=1))
    for iteration in range(ITERS):
        kernel_image = apply(direction.astype(jnp.bfloat16))
        step_size = norm_now / lax.optimization_barrier(jnp.sum(direction * kernel_image, axis=1))
        solution = solution + step_size[:, None] * direction
        residual = residual - step_size[:, None] * kernel_image
        if iteration + 1 < ITERS:
            norm_next = lax.optimization_barrier(jnp.sum(residual * residual, axis=1))
            direction = residual + (norm_next / norm_now)[:, None] * direction
            norm_now = norm_next
    return (solution, residual)
```

```python
import functools

import jax
import jax.numpy as jnp
from jax import lax
from jax.experimental import pallas as pl
from jax.experimental.pallas import tpu as pltpu
from jax.sharding import PartitionSpec as P

f32 = jnp.float32
bf16 = jnp.bfloat16

SQRT_THREE = 1.7320508075688772
NOISE_VAR = 1.0

RANK = 32
PROBES = 128
POINTS = 1024
PLANE = 32
DEPTH = 16
ROWS = 24
Z_ROWS = 16
LEAST = 384
MOST = 640

NT = (((1,), (1,)), ((), ()))
TN = (((0,), (0,)), ((), ()))
NN = (((1,), (0,)), ((), ()))


def first_row(level):
    if level < 5:
        return 2 * (level - 1)
    return 16 if level == 5 else 8 + 2 * (level - 6)


def dot(a, b, dims):
    return lax.dot_general(a, b, dims, preferred_element_type=f32)


def halves(x):
    high = x.astype(bf16)
    return high, (x - high.astype(f32)).astype(bf16)


def dot_split(a, b, dims):
    a_high, a_low = halves(a)
    b_high, b_low = halves(b)
    a_dim, b_dim = dims[0][0][0], dims[0][1][0]
    return dot(
        jnp.concatenate([a_high, a_high, a_low], axis=a_dim),
        jnp.concatenate([b_high, b_low, b_high], axis=b_dim),
        dims,
    )


def rows_of(products):
    part = products[:, :PROBES]
    for start in range(PROBES, POINTS, PROBES):
        part = part + products[:, start : start + PROBES]
    return jnp.sum(part.T, axis=0, keepdims=True)


def down_rows(row):
    square = jnp.broadcast_to(row, (PROBES, PROBES)).T
    return jnp.concatenate([square] * (POINTS // PROBES), axis=1)


def row_ids(rows):
    return lax.broadcasted_iota(jnp.int32, (rows, PROBES), 0)


def send_levels(rounded, basis_ref, coupling_ref, send_ref):
    wide = basis_ref[1:10].reshape(9 * RANK, POINTS)
    projected = dot(wide, rounded, NT)
    for level in range(1, 10):
        own = coupling_ref[0, level, :RANK, :]
        partial = dot_split(own, projected[RANK * (level - 1) : RANK * level], TN)
        for half in range(2):
            send_ref[pl.ds(first_row(level) + half, PLANE, stride=ROWS), :] = partial[
                PLANE * half : PLANE * (half + 1)
            ]
    blank = jnp.zeros((PLANE, PROBES), f32)
    for row in range(18, ROWS):
        send_ref[pl.ds(row, PLANE, stride=ROWS), :] = blank


def start_kernel(right_ref, basis_ref, coupling_ref, send_ref):
    send_levels(right_ref[...].astype(bf16), basis_ref, coupling_ref, send_ref)


def leaf_level(v, rounded, boundary, tile, basis_ref, coupling_ref):
    leaf = dot(rounded, tile, NN)
    wide = basis_ref[0].astype(f32)
    in_first = lax.broadcasted_iota(jnp.int32, (RANK, POINTS), 1) < boundary
    both = jnp.concatenate(
        [jnp.where(in_first, wide, 0.0), jnp.where(in_first, 0.0, wide)], axis=0
    ).astype(bf16)
    factor = coupling_ref[0, 0]
    mixed = dot_split(factor, dot(both, rounded, NT), TN)
    coefficients = dot_split(factor, mixed, NN).astype(bf16)
    image = leaf + dot(coefficients, both, TN)
    curvature = rows_of(v * leaf) + jnp.sum(mixed * mixed, axis=0, keepdims=True)
    return image, curvature


def tile_kernel(
    coordinates_ref, order_ref, sizes_ref, right_ref, basis_ref, coupling_ref,
    tile_ref, image_ref, scalars_ref, pick_ref, column_ref,
):
    boundary = sizes_ref[0, 0]
    order = order_ref[...]
    step = 128

    @pl.loop(0, POINTS // step)
    def _(block):
        start = pl.multiple_of(block * step, step)
        ids = start + lax.broadcasted_iota(jnp.int32, (step, POINTS), 0)
        pick_ref[pl.ds(start, step), :] = jnp.where(ids == order, 1.0, 0.0).astype(bf16)

    whole = coordinates_ref[...]
    high = whole.astype(bf16).astype(f32)
    middle = (whole - high).astype(bf16).astype(f32)
    low = whole - high - middle
    terms = jnp.concatenate([high, middle, low], axis=0).astype(bf16)
    picked = dot(terms, pick_ref[...], NN)
    x = (picked[0:3] + picked[3:6]) + picked[6:9]
    column_ref[...] = jnp.concatenate([x, jnp.zeros((5, POINTS), f32)], axis=0).T

    def fill(row_start, row_stop, col_start, col_stop):
        group = 16
        width = col_stop - col_start
        across = [x[c : c + 1, col_start:col_stop] for c in range(3)]
        col_ids = col_start + lax.broadcasted_iota(jnp.int32, (group, width), 1)
        col_first = col_ids < boundary

        @pl.loop(0, (row_stop - row_start) // group)
        def _(block):
            start = pl.multiple_of(row_start + block * group, group)
            down = column_ref[pl.ds(start, group), :]
            dist_sq = jnp.zeros((group, width), f32)
            for c in range(3):
                offset = down[:, c : c + 1] - across[c]
                dist_sq = dist_sq + offset * offset
            scaled = SQRT_THREE * jnp.sqrt(dist_sq)
            values = (1.0 + scaled) * jnp.exp(-scaled)
            ids = start + lax.broadcasted_iota(jnp.int32, (group, width), 0)
            limit = jnp.where(ids < boundary, 0, boundary)
            low_end = jnp.where(ids < boundary, boundary, POINTS)
            same = (col_ids >= limit) & (col_ids < low_end)
            values = jnp.where(same, values, 0.0) + jnp.where(ids == col_ids, NOISE_VAR, 0.0)
            tile_ref[pl.ds(start, group), col_start:col_stop] = values.astype(bf16)

    tile_ref[:LEAST, MOST:] = jnp.zeros((LEAST, POINTS - MOST), bf16)
    tile_ref[MOST:, :LEAST] = jnp.zeros((POINTS - MOST, LEAST), bf16)
    fill(0, LEAST, 0, MOST)
    fill(LEAST, MOST, 0, POINTS)
    fill(MOST, POINTS, LEAST, POINTS)

    v = right_ref[...]
    image, curvature = leaf_level(
        v, v.astype(bf16), boundary, tile_ref[...], basis_ref, coupling_ref
    )
    image_ref[...] = image
    scalars_ref[...] = jnp.concatenate(
        [jnp.zeros((2, PROBES), f32), curvature, rows_of(v * v), jnp.zeros((4, PROBES), f32)],
        axis=0,
    )


def leaf_kernel(
    sizes_ref, residual_ref, first_image_ref, tile_ref, basis_ref, coupling_ref,
    image_ref, scalars_ref,
):
    v = residual_ref[...]
    image, curvature = leaf_level(
        v, v.astype(bf16), sizes_ref[0, 0], tile_ref[...], basis_ref, coupling_ref
    )
    image_ref[...] = image
    scalars_ref[...] = jnp.concatenate(
        [
            jnp.zeros((2, PROBES), f32),
            curvature,
            rows_of(v * v),
            rows_of(v * first_image_ref[...]),
            jnp.zeros((3, PROBES), f32),
        ],
        axis=0,
    )


def pair_sums(got_ref):
    sums = [[got_ref[ROWS * d : ROWS * d + 8, :] for d in range(PLANE)]]
    for _ in range(4):
        last = sums[-1]
        sums.append([last[2 * i] + last[2 * i + 1] for i in range(len(last) // 2)])
    return sums


def total(got_ref, count, rows, start):
    parts = [got_ref[rows * d + start : rows * d + start + 8, :] for d in range(count)]
    while len(parts) > 1:
        parts = [parts[2 * i] + parts[2 * i + 1] for i in range(len(parts) // 2)]
    return parts[0]


def squares(nodes):
    result = nodes[0] * nodes[0]
    for node in nodes[1:]:
        result = result + node * node
    return result


def plane_kernel(got_ref, scalars_ref, send_ref):
    ids = row_ids(8)
    sums = pair_sums(got_ref)
    square = jnp.zeros((8, PROBES), f32)
    for level in range(1, 5):
        square = jnp.where(ids // 2 == level - 1, squares(sums[level]), square)
    fifth = total(got_ref, PLANE, ROWS, 16)
    square = square + jnp.where(ids < 2, fifth * fifth, 0.0)
    curvature = jnp.sum(square, axis=0, keepdims=True)
    scalars = scalars_ref[...] + jnp.where(ids == 2, curvature, 0.0)
    upper = total(got_ref, PLANE, ROWS, 8)
    for z in range(DEPTH):
        send_ref[Z_ROWS * z : Z_ROWS * z + 8, :] = upper
        send_ref[Z_ROWS * z + 8 : Z_ROWS * (z + 1), :] = scalars


def depth_kernel(got_ref, z_got_ref, send_ref):
    own = lax.axis_index("pts") // PLANE
    ids = row_ids(8)
    reach = jnp.left_shift(2, ids // 2)
    pair = jnp.zeros((8, PROBES), f32)
    nodes = []
    for z in range(DEPTH):
        block = z_got_ref[Z_ROWS * z : Z_ROWS * z + 8, :]
        nodes.append(block)
        apart = jnp.bitwise_xor(own, z)
        pair = pair + jnp.where(apart < reach, block, 0.0)
    square = jnp.zeros((8, PROBES), f32)
    for level in range(4):
        nodes = [nodes[2 * i] + nodes[2 * i + 1] for i in range(len(nodes) // 2)]
        square = jnp.where(ids // 2 == level, squares(nodes), square)
    curvature = jnp.sum(square, axis=0, keepdims=True)
    scalars = total(z_got_ref, DEPTH, Z_ROWS, 8) + jnp.where(ids == 2, curvature, 0.0)
    fifth = total(got_ref, PLANE, ROWS, 16)
    last = jnp.where(ids < 2, fifth, scalars)
    sums = pair_sums(got_ref)
    for d in range(PLANE):
        first = sums[4][d >> 4]
        for level in (3, 2, 1):
            first = jnp.where(ids // 2 == level - 1, sums[level][d >> level], first)
        send_ref[ROWS * d : ROWS * d + 8, :] = first
        send_ref[ROWS * d + 8 : ROWS * d + 16, :] = pair
        send_ref[ROWS * d + 16 : ROWS * d + 24, :] = last


def expand(got_ref, basis_ref, coupling_ref):
    coefficients = []
    for level in range(1, 10):
        mixed = jnp.concatenate(
            [
                got_ref[pl.ds(first_row(level) + half, PLANE, stride=ROWS), :]
                for half in range(2)
            ],
            axis=0,
        )
        coefficients.append(dot_split(coupling_ref[0, level, :RANK, :], mixed, NN))
    narrow = jnp.concatenate(coefficients, axis=0).astype(bf16)
    return dot(narrow, basis_ref[1:10].reshape(9 * RANK, POINTS), TN)


def turn_kernel(
    got_ref, right_ref, image_ref, basis_ref, coupling_ref,
    residual_ref, whole_image_ref, send_ref, keep_ref,
):
    scalars = total(got_ref, PLANE, ROWS, 16)
    curvature, norm = scalars[2:3], scalars[3:4]
    step = norm / curvature
    whole = image_ref[...] + expand(got_ref, basis_ref, coupling_ref)
    residual = right_ref[...] - down_rows(step) * whole
    whole_image_ref[...] = whole
    residual_ref[...] = residual
    keep_ref[...] = jnp.concatenate(
        [step, curvature, norm, jnp.zeros((5, PROBES), f32)], axis=0
    )
    send_levels(residual.astype(bf16), basis_ref, coupling_ref, send_ref)


def end_kernel(
    got_ref, right_ref, residual_ref, first_image_ref, image_ref, basis_ref, coupling_ref,
    keep_ref, solution_ref, last_ref,
):
    scalars = total(got_ref, PLANE, ROWS, 16)
    own, norm, cross = scalars[2:3], scalars[3:4], scalars[4:5]
    step, curvature, norm_before = keep_ref[0:1, :], keep_ref[1:2, :], keep_ref[2:3, :]
    ratio = norm / norm_before
    step_now = norm / (own + 2.0 * ratio * cross + ratio * ratio * curvature)
    ratio_down, step_down = down_rows(ratio), down_rows(step_now)
    right, residual = right_ref[...], residual_ref[...]
    direction = residual + ratio_down * right
    solution_ref[...] = down_rows(step) * right + step_down * direction
    image = image_ref[...] + expand(got_ref, basis_ref, coupling_ref)
    last_ref[...] = residual - step_down * (image + ratio_down * first_image_ref[...])


VMEM = pl.BlockSpec(memory_space=pltpu.VMEM)
SMEM = pl.BlockSpec(memory_space=pltpu.SMEM)


def call(body, outs, ins, megabytes, cost, scratch=(), name=None):
    specs = [SMEM if a.dtype == jnp.int32 and a.shape == (1, 2) else VMEM for a in ins]
    return pl.pallas_call(
        body,
        out_shape=[jax.ShapeDtypeStruct(shape, kind) for shape, kind in outs],
        in_specs=specs,
        out_specs=[VMEM] * len(outs),
        scratch_shapes=list(scratch),
        compiler_params=pltpu.CompilerParams(vmem_limit_bytes=megabytes << 20),
        cost_estimate=pl.CostEstimate(flops=cost, bytes_accessed=2 << 20, transcendentals=0),
        name=name,
    )(*ins)


def plane_groups(count):
    return [list(range(PLANE * z, PLANE * (z + 1))) for z in range(count // PLANE)]


def depth_groups(count):
    return [list(range(place, count, PLANE)) for place in range(PLANE)]


def exchange(rows, groups):
    members = len(groups[0])
    blocks = rows.reshape(members, rows.shape[0] // members, PROBES)
    got = lax.all_to_all(blocks, "pts", 0, 0, axis_index_groups=groups)
    return got.reshape(rows.shape)


def on_device(right_side, coordinates, tree_order, leaf_sizes, level_basis, coupling):
    count = lax.axis_size("pts")
    planes, depths = plane_groups(count), depth_groups(count)
    field = ((PROBES, POINTS), f32)
    message = ((PLANE * ROWS, PROBES), f32)
    z_message = ((DEPTH * Z_ROWS, PROBES), f32)
    row_block = ((8, PROBES), f32)

    def tree(send, scalars_of):
        got = exchange(send, planes)
        local = scalars_of()
        (z_send,) = call(plane_kernel, [z_message], [got, local[-1]], 8, 1 << 20, name="plane")
        z_got = exchange(z_send, depths)
        (back,) = call(depth_kernel, [message], [got, z_got], 8, 1 << 20, name="depth")
        return local, exchange(back, planes)

    (send,) = call(
        start_kernel, [message], [right_side, level_basis, coupling], 16, 1 << 26, name="start"
    )
    (tile, image, _), got = tree(
        send,
        lambda: call(
            tile_kernel,
            [((POINTS, POINTS), bf16), field, row_block],
            [coordinates, tree_order, leaf_sizes, right_side, level_basis, coupling],
            24,
            4 << 30,
            scratch=[pltpu.VMEM((POINTS, POINTS), bf16), pltpu.VMEM((POINTS, 8), f32)],
            name="tile",
        ),
    )
    residual, first_image, send, keep = call(
        turn_kernel,
        [field, field, message, row_block],
        [got, right_side, image, level_basis, coupling],
        16,
        1 << 28,
        name="turn",
    )
    (image, _), got = tree(
        send,
        lambda: call(
            leaf_kernel,
            [field, row_block],
            [leaf_sizes, residual, first_image, tile, level_basis, coupling],
            24,
            1 << 30,
            name="leaf",
        ),
    )
    return tuple(
        call(
            end_kernel,
            [field, field],
            [got, right_side, residual, first_image, image, level_basis, coupling, keep],
            16,
            1 << 28,
            name="end",
        )
    )


def solution(mesh):
    in_specs = (
        P(None, "pts"),
        P(None, "pts"),
        P("pts", None),
        P("pts", None),
        P(None, None, "pts"),
        P("pts", None, None, None),
    )
    out_specs = (P(None, "pts"), P(None, "pts"))
    return jax.shard_map(
        on_device, mesh=mesh, in_specs=in_specs, out_specs=out_specs, check_vma=False
    )
```

```python
import functools

import jax
import jax.numpy as jnp
from jax import lax
from jax.experimental import pallas as pl
from jax.experimental.pallas import tpu as pltpu
from jax.sharding import PartitionSpec as P

f32 = jnp.float32
bf16 = jnp.bfloat16

SQRT_THREE = 1.7320508075688772
NOISE_VAR = 1.0

RANK = 32
PROBES = 128
POINTS = 1024
PLANE = 32
DEPTH = 16
ROWS = 18
BACK = 21
Z_ROWS = 11
LEAST = 384
MOST = 640

NT = (((1,), (1,)), ((), ()))
TN = (((0,), (0,)), ((), ()))
NN = (((1,), (0,)), ((), ()))


def first_row(level):
    if level < 5:
        return 2 * (level - 1)
    return 16 if level == 5 else 8 + 2 * (level - 6)


def dot(a, b, dims):
    return lax.dot_general(a, b, dims, preferred_element_type=f32)


def halves(x):
    high = x.astype(bf16)
    return high, (x - high.astype(f32)).astype(bf16)


def dot_split(a, b, dims):
    a_high, a_low = halves(a)
    b_high, b_low = halves(b)
    a_dim, b_dim = dims[0][0][0], dims[0][1][0]
    return dot(
        jnp.concatenate([a_high, a_high, a_low], axis=a_dim),
        jnp.concatenate([b_high, b_low, b_high], axis=b_dim),
        dims,
    )


def rows_of(products):
    part = products[:, :PROBES]
    for start in range(PROBES, POINTS, PROBES):
        part = part + products[:, start : start + PROBES]
    return jnp.sum(part.T, axis=0, keepdims=True)


def down_rows(row):
    square = jnp.broadcast_to(row, (PROBES, PROBES)).T
    return jnp.concatenate([square] * (POINTS // PROBES), axis=1)


def row_ids(rows):
    return lax.broadcasted_iota(jnp.int32, (rows, PROBES), 0)


def send_levels(rounded, basis_ref, coupling_ref, send_ref):
    wide = basis_ref[1:10].reshape(9 * RANK, POINTS)
    projected = dot(wide, rounded, NT)
    for level in range(1, 10):
        own = coupling_ref[0, level, :RANK, :]
        partial = dot_split(own, projected[RANK * (level - 1) : RANK * level], TN)
        for half in range(2):
            send_ref[pl.ds(first_row(level) + half, PLANE, stride=ROWS), :] = partial[
                PLANE * half : PLANE * (half + 1)
            ]


def start_kernel(
    right_hbm, basis_hbm, coupling_hbm, send_hbm,
    right_ref, basis_ref, coupling_ref, send_ref, sems,
):
    copies = [
        pltpu.make_async_copy(right_hbm, right_ref, sems.at[0]),
        pltpu.make_async_copy(basis_hbm, basis_ref, sems.at[1]),
        pltpu.make_async_copy(coupling_hbm, coupling_ref, sems.at[2]),
    ]
    for copy in copies:
        copy.start()
    for copy in copies:
        copy.wait()
    send_levels(right_ref[...].astype(bf16), basis_ref, coupling_ref, send_ref)
    out = pltpu.make_async_copy(send_ref, send_hbm, sems.at[3])
    out.start()
    out.wait()


def leaf_level(v, rounded, boundary, tile, basis_ref, coupling_ref):
    leaf = dot(rounded, tile, NN)
    wide = basis_ref[0].astype(f32)
    in_first = lax.broadcasted_iota(jnp.int32, (RANK, POINTS), 1) < boundary
    both = jnp.concatenate(
        [jnp.where(in_first, wide, 0.0), jnp.where(in_first, 0.0, wide)], axis=0
    ).astype(bf16)
    factor = coupling_ref[0, 0]
    mixed = dot_split(factor, dot(both, rounded, NT), TN)
    coefficients = dot_split(factor, mixed, NN).astype(bf16)
    image = leaf + dot(coefficients, both, TN)
    curvature = rows_of(v * leaf) + jnp.sum(mixed * mixed, axis=0, keepdims=True)
    return image, curvature


def tile_kernel(
    coordinates_ref, order_ref, sizes_ref, right_ref, basis_ref, coupling_ref,
    tile_ref, image_ref, scalars_ref, down_ref,
):
    boundary = sizes_ref[0, 0]
    order = order_ref[...]
    place, segment = jnp.bitwise_and(order, 127), jnp.right_shift(order, 7)
    sources = [
        jnp.concatenate(
            [coordinates_ref[:, start : start + 128], jnp.zeros((5, 128), f32)], axis=0
        )
        for start in range(0, POINTS, 128)
    ]
    pieces = []
    for start in range(0, POINTS, 128):
        lane = jnp.broadcast_to(place[:, start : start + 128], (8, 128))
        chosen = jnp.broadcast_to(segment[:, start : start + 128], (8, 128))
        piece = jnp.zeros((8, 128), f32)
        for number, source in enumerate(sources):
            piece = jnp.where(chosen == number, jnp.take_along_axis(source, lane, axis=1), piece)
        pieces.append(piece)
    x = jnp.concatenate(pieces, axis=1)
    column = x.T
    for c in range(3):
        down_ref[c] = jnp.broadcast_to(column[:, c : c + 1], (POINTS, 128))
    edge = boundary.astype(f32) - 0.5

    def fill(row_start, row_stop, col_start, col_stop):
        group = 128
        width = col_stop - col_start
        across = [x[c : c + 1, col_start:col_stop] for c in range(3)]
        col_ids = col_start + lax.broadcasted_iota(jnp.int32, (1, width), 1)
        col_side = col_ids.astype(f32) - edge

        def widen(block):
            return jnp.concatenate([block] * (width // 128), axis=1)

        @pl.loop(0, (row_stop - row_start) // group)
        def _(block):
            start = pl.multiple_of(row_start + block * group, group)
            dist_sq = None
            for c in range(3):
                offset = widen(down_ref[c, pl.ds(start, group), :]) - across[c]
                dist_sq = offset * offset if c == 0 else dist_sq + offset * offset
            root = dist_sq * lax.rsqrt(jnp.maximum(dist_sq, 1e-37))
            scaled = SQRT_THREE * root
            values = (1.0 + scaled) * jnp.exp(-scaled)
            ids = start + lax.broadcasted_iota(jnp.int32, (group, 128), 0)
            same = widen(ids.astype(f32) - edge) * col_side > 0.0
            values = jnp.where(same, values, 0.0)
            values = values + jnp.where(widen(ids) == col_ids, NOISE_VAR, 0.0)
            tile_ref[pl.ds(start, group), col_start:col_stop] = values.astype(bf16)

    tile_ref[:LEAST, MOST:] = jnp.zeros((LEAST, POINTS - MOST), bf16)
    tile_ref[MOST:, :LEAST] = jnp.zeros((POINTS - MOST, LEAST), bf16)
    fill(0, LEAST, 0, MOST)
    fill(LEAST, MOST, 0, POINTS)
    fill(MOST, POINTS, LEAST, POINTS)

    v = right_ref[...]
    image, curvature = leaf_level(
        v, v.astype(bf16), boundary, tile_ref[...], basis_ref, coupling_ref
    )
    image_ref[...] = image
    scalars_ref[...] = jnp.concatenate(
        [curvature, rows_of(v * v), jnp.zeros((6, PROBES), f32)], axis=0
    )


def leaf_kernel(
    sizes_ref, residual_ref, first_image_ref, tile_ref, basis_ref, coupling_ref,
    image_ref, scalars_ref,
):
    v = residual_ref[...]
    image, curvature = leaf_level(
        v, v.astype(bf16), sizes_ref[0, 0], tile_ref[...], basis_ref, coupling_ref
    )
    image_ref[...] = image
    scalars_ref[...] = jnp.concatenate(
        [
            curvature,
            rows_of(v * v),
            rows_of(v * first_image_ref[...]),
            jnp.zeros((5, PROBES), f32),
        ],
        axis=0,
    )


def pair_sums(got_ref):
    sums = [[got_ref[ROWS * d : ROWS * d + 8, :] for d in range(PLANE)]]
    for _ in range(4):
        last = sums[-1]
        sums.append([last[2 * i] + last[2 * i + 1] for i in range(len(last) // 2)])
    return sums


def total(got_ref, count, stride, start, rows):
    parts = [got_ref[stride * d + start : stride * d + start + rows, :] for d in range(count)]
    while len(parts) > 1:
        parts = [parts[2 * i] + parts[2 * i + 1] for i in range(len(parts) // 2)]
    return parts[0]


def squares(nodes):
    result = nodes[0] * nodes[0]
    for node in nodes[1:]:
        result = result + node * node
    return result


def plane_kernel(got_ref, scalars_ref, send_ref):
    ids = row_ids(8)
    sums = pair_sums(got_ref)
    square = jnp.zeros((8, PROBES), f32)
    for level in range(1, 5):
        square = jnp.where(ids // 2 == level - 1, squares(sums[level]), square)
    fifth = total(got_ref, PLANE, ROWS, 16, 2)
    curvature = jnp.sum(square, axis=0, keepdims=True) + jnp.sum(
        fifth * fifth, axis=0, keepdims=True
    )
    scalars = scalars_ref[0:3, :] + jnp.where(row_ids(3) == 0, curvature, 0.0)
    block = jnp.concatenate([total(got_ref, PLANE, ROWS, 8, 8), scalars], axis=0)
    for z in range(DEPTH):
        send_ref[Z_ROWS * z : Z_ROWS * (z + 1), :] = block


def depth_kernel(got_ref, z_got_ref, send_ref):
    own = lax.axis_index("pts") // PLANE
    ids = row_ids(8)
    reach = jnp.left_shift(2, ids // 2)
    pair = jnp.zeros((8, PROBES), f32)
    nodes = []
    for z in range(DEPTH):
        block = z_got_ref[Z_ROWS * z : Z_ROWS * z + 8, :]
        nodes.append(block)
        apart = jnp.bitwise_xor(own, z)
        pair = pair + jnp.where(apart < reach, block, 0.0)
    square = jnp.zeros((8, PROBES), f32)
    for level in range(4):
        nodes = [nodes[2 * i] + nodes[2 * i + 1] for i in range(len(nodes) // 2)]
        square = jnp.where(ids // 2 == level, squares(nodes), square)
    curvature = jnp.sum(square, axis=0, keepdims=True)
    scalars = total(z_got_ref, DEPTH, Z_ROWS, 8, 3)
    scalars = scalars + jnp.where(row_ids(3) == 0, curvature, 0.0)
    tail = jnp.concatenate([pair, total(got_ref, PLANE, ROWS, 16, 2), scalars], axis=0)
    sums = pair_sums(got_ref)
    for d in range(PLANE):
        first = sums[4][d >> 4]
        for level in (3, 2, 1):
            first = jnp.where(ids // 2 == level - 1, sums[level][d >> level], first)
        send_ref[BACK * d : BACK * d + 8, :] = first
        send_ref[BACK * d + 8 : BACK * (d + 1), :] = tail


def expand(got_ref, basis_ref, coupling_ref):
    coefficients = []
    for level in range(1, 10):
        mixed = jnp.concatenate(
            [
                got_ref[pl.ds(first_row(level) + half, PLANE, stride=BACK), :]
                for half in range(2)
            ],
            axis=0,
        )
        coefficients.append(dot_split(coupling_ref[0, level, :RANK, :], mixed, NN))
    narrow = jnp.concatenate(coefficients, axis=0).astype(bf16)
    return dot(narrow, basis_ref[1:10].reshape(9 * RANK, POINTS), TN)


def turn_kernel(
    got_ref, right_ref, image_ref, basis_ref, coupling_ref,
    residual_ref, whole_image_ref, send_hbm, keep_ref, send_ref, sem,
):
    scalars = total(got_ref, PLANE, BACK, 18, 3)
    curvature, norm = scalars[0:1], scalars[1:2]
    step = norm / curvature
    whole = image_ref[...] + expand(got_ref, basis_ref, coupling_ref)
    residual = right_ref[...] - down_rows(step) * whole
    whole_image_ref[...] = whole
    residual_ref[...] = residual
    keep_ref[...] = jnp.concatenate(
        [step, curvature, norm, jnp.zeros((5, PROBES), f32)], axis=0
    )
    send_levels(residual.astype(bf16), basis_ref, coupling_ref, send_ref)
    out = pltpu.make_async_copy(send_ref, send_hbm, sem.at[0])
    out.start()
    out.wait()


def end_kernel(
    got_ref, right_ref, residual_ref, first_image_ref, image_ref, basis_ref, coupling_ref,
    keep_ref, solution_ref, last_ref,
):
    scalars = total(got_ref, PLANE, BACK, 18, 3)
    own, norm, cross = scalars[0:1], scalars[1:2], scalars[2:3]
    step, curvature, norm_before = keep_ref[0:1, :], keep_ref[1:2, :], keep_ref[2:3, :]
    ratio = norm / norm_before
    step_now = norm / (own + 2.0 * ratio * cross + ratio * ratio * curvature)
    ratio_down, step_down = down_rows(ratio), down_rows(step_now)
    right, residual = right_ref[...], residual_ref[...]
    direction = residual + ratio_down * right
    solution_ref[...] = down_rows(step) * right + step_down * direction
    image = image_ref[...] + expand(got_ref, basis_ref, coupling_ref)
    last_ref[...] = residual - step_down * (image + ratio_down * first_image_ref[...])


VMEM = pl.BlockSpec(memory_space=pltpu.VMEM)
SMEM = pl.BlockSpec(memory_space=pltpu.SMEM)
HBM = pl.BlockSpec(memory_space=pltpu.HBM)


def call(body, outs, ins, megabytes, cost, scratch=(), name=None, far_ins=(), far_outs=()):
    specs = [SMEM if a.dtype == jnp.int32 and a.shape == (1, 2) else VMEM for a in ins]
    for place in far_ins:
        specs[place] = HBM
    return pl.pallas_call(
        body,
        out_shape=[jax.ShapeDtypeStruct(shape, kind) for shape, kind in outs],
        in_specs=specs,
        out_specs=[HBM if place in far_outs else VMEM for place in range(len(outs))],
        scratch_shapes=list(scratch),
        compiler_params=pltpu.CompilerParams(vmem_limit_bytes=megabytes << 20),
        cost_estimate=pl.CostEstimate(flops=cost, bytes_accessed=2 << 20, transcendentals=0),
        name=name,
    )(*ins)


def plane_groups(count):
    return [list(range(PLANE * z, PLANE * (z + 1))) for z in range(count // PLANE)]


def depth_groups(count):
    return [list(range(place, count, PLANE)) for place in range(PLANE)]


def exchange(rows, groups):
    members = len(groups[0])
    blocks = rows.reshape(members, 1, rows.shape[0] // members * PROBES)
    got = lax.all_to_all(blocks, "pts", 0, 0, axis_index_groups=groups)
    return got.reshape(rows.shape)


def on_device(right_side, coordinates, tree_order, leaf_sizes, level_basis, coupling):
    count = lax.axis_size("pts")
    planes, depths = plane_groups(count), depth_groups(count)
    field = ((PROBES, POINTS), f32)
    message = ((PLANE * ROWS, PROBES), f32)
    back_message = ((PLANE * BACK, PROBES), f32)
    z_message = ((DEPTH * Z_ROWS, PROBES), f32)
    row_block = ((8, PROBES), f32)
    message_scratch = pltpu.VMEM(*message)

    def tree(send, scalars_of):
        got = exchange(send, planes)
        local = scalars_of()
        (z_send,) = call(plane_kernel, [z_message], [got, local[-1]], 2, 1 << 20, name="plane")
        z_got = exchange(z_send, depths)
        (back,) = call(depth_kernel, [back_message], [got, z_got], 2, 1 << 20, name="depth")
        return local, exchange(back, planes)

    (send,) = call(
        start_kernel,
        [message],
        [right_side, level_basis, coupling],
        60,
        1 << 26,
        scratch=[
            pltpu.VMEM(right_side.shape, f32),
            pltpu.VMEM(level_basis.shape, bf16),
            pltpu.VMEM(coupling.shape, f32),
            message_scratch,
            pltpu.SemaphoreType.DMA((4,)),
        ],
        name="start",
        far_ins=(0, 1, 2),
        far_outs=(0,),
    )
    (tile, image, _), got = tree(
        send,
        lambda: call(
            tile_kernel,
            [((POINTS, POINTS), bf16), field, row_block],
            [coordinates, tree_order, leaf_sizes, right_side, level_basis, coupling],
            12,
            4 << 30,
            scratch=[pltpu.VMEM((3, POINTS, 128), f32)],
            name="tile",
        ),
    )
    residual, first_image, send, keep = call(
        turn_kernel,
        [field, field, message, row_block],
        [got, right_side, image, level_basis, coupling],
        8,
        1 << 28,
        scratch=[message_scratch, pltpu.SemaphoreType.DMA((1,))],
        name="turn",
        far_outs=(2,),
    )
    (image, _), got = tree(
        send,
        lambda: call(
            leaf_kernel,
            [field, row_block],
            [leaf_sizes, residual, first_image, tile, level_basis, coupling],
            8,
            1 << 30,
            name="leaf",
        ),
    )
    return tuple(
        call(
            end_kernel,
            [field, field],
            [got, right_side, residual, first_image, image, level_basis, coupling, keep],
            8,
            1 << 28,
            name="end",
        )
    )


def solution(mesh):
    in_specs = (
        P(None, "pts"),
        P(None, "pts"),
        P("pts", None),
        P("pts", None),
        P(None, None, "pts"),
        P("pts", None, None, None),
    )
    out_specs = (P(None, "pts"), P(None, "pts"))
    return jax.shard_map(
        on_device, mesh=mesh, in_specs=in_specs, out_specs=out_specs, check_vma=False
    )
```

```python
import functools

import jax
import jax.numpy as jnp
from jax import lax
from jax.experimental import pallas as pl
from jax.experimental.pallas import tpu as pltpu
from jax.sharding import PartitionSpec as P

f32 = jnp.float32
bf16 = jnp.bfloat16

SQRT_THREE = 1.7320508075688772
NOISE_VAR = 1.0

RANK = 32
PROBES = 128
POINTS = 1024
PLANE = 32
DEPTH = 16
ROWS = 18
BACK = 21
Z_ROWS = 11
LEAST = 384
MOST = 640
HALVES = 2

NT = (((1,), (1,)), ((), ()))
TN = (((0,), (0,)), ((), ()))
NN = (((1,), (0,)), ((), ()))


def first_row(level):
    if level < 5:
        return 2 * (level - 1)
    return 16 if level == 5 else 8 + 2 * (level - 6)


def dot(a, b, dims):
    return lax.dot_general(a, b, dims, preferred_element_type=f32)


def halves(x):
    high = x.astype(bf16)
    return high, (x - high.astype(f32)).astype(bf16)


def dot_split(a, b, dims):
    a_high, a_low = halves(a)
    b_high, b_low = halves(b)
    a_dim, b_dim = dims[0][0][0], dims[0][1][0]
    return dot(
        jnp.concatenate([a_high, a_high, a_low], axis=a_dim),
        jnp.concatenate([b_high, b_low, b_high], axis=b_dim),
        dims,
    )


def rows_of(products):
    part = products[:, :PROBES]
    for start in range(PROBES, POINTS, PROBES):
        part = part + products[:, start : start + PROBES]
    return jnp.sum(part.T, axis=0, keepdims=True)


def down_rows(row):
    square = jnp.broadcast_to(row, (PROBES, PROBES)).T
    return jnp.concatenate([square] * (POINTS // PROBES), axis=1)


def row_ids(rows):
    return lax.broadcasted_iota(jnp.int32, (rows, PROBES), 0)


def send_levels(projected, coupling_ref, send_ref):
    for level in range(1, 10):
        own = coupling_ref[0, level, :RANK, :]
        partial = dot_split(own, projected[RANK * (level - 1) : RANK * level], TN)
        for half in range(2):
            send_ref[pl.ds(first_row(level) + half, PLANE, stride=ROWS), :] = partial[
                PLANE * half : PLANE * (half + 1)
            ]


def start_kernel(
    right_hbm, basis_hbm, coupling_hbm, send_hbm,
    right_ref, basis_ref, coupling_ref, send_ref, sems,
):
    width = POINTS // HALVES
    fetches = []
    for half in range(HALVES):
        span = pl.ds(width * half, width)
        right_copy = pltpu.make_async_copy(
            right_hbm.at[:, span], right_ref.at[:, span], sems.at[2 * half]
        )
        basis_copy = pltpu.make_async_copy(
            basis_hbm.at[pl.ds(1, 9), :, span],
            basis_ref.at[:, :, span],
            sems.at[2 * half + 1],
        )
        right_copy.start()
        basis_copy.start()
        fetches.append((right_copy, basis_copy))
    factors = pltpu.make_async_copy(coupling_hbm, coupling_ref, sems.at[2 * HALVES])
    factors.start()
    projected = None
    for half, (right_copy, basis_copy) in enumerate(fetches):
        span = slice(width * half, width * (half + 1))
        right_copy.wait()
        basis_copy.wait()
        part = dot(
            basis_ref[:, :, span].reshape(9 * RANK, width),
            right_ref[:, span].astype(bf16),
            NT,
        )
        projected = part if half == 0 else projected + part
    factors.wait()
    send_levels(projected, coupling_ref, send_ref)
    out = pltpu.make_async_copy(send_ref, send_hbm, sems.at[2 * HALVES + 1])
    out.start()
    out.wait()


def leaf_level(v, rounded, leaf, boundary, basis_ref, coupling_ref):
    wide = basis_ref[0].astype(f32)
    in_first = lax.broadcasted_iota(jnp.int32, (RANK, POINTS), 1) < boundary
    both = jnp.concatenate(
        [jnp.where(in_first, wide, 0.0), jnp.where(in_first, 0.0, wide)], axis=0
    ).astype(bf16)
    factor = coupling_ref[0, 0]
    mixed = dot_split(factor, dot(both, rounded, NT), TN)
    coefficients = dot_split(factor, mixed, NN).astype(bf16)
    image = leaf + dot(coefficients, both, TN)
    curvature = rows_of(v * leaf) + jnp.sum(mixed * mixed, axis=0, keepdims=True)
    return image, curvature


def tile_kernel(
    coordinates_ref, order_ref, sizes_ref, right_ref, basis_ref, coupling_ref,
    tile_hbm, image_ref, scalars_ref, tile_ref, down_ref, sems,
):
    boundary = sizes_ref[0, 0]
    order = order_ref[...]
    place, segment = jnp.bitwise_and(order, 127), jnp.right_shift(order, 7)
    sources = [
        jnp.concatenate(
            [coordinates_ref[:, start : start + 128], jnp.zeros((5, 128), f32)], axis=0
        )
        for start in range(0, POINTS, 128)
    ]
    pieces = []
    for start in range(0, POINTS, 128):
        lane = jnp.broadcast_to(place[:, start : start + 128], (8, 128))
        chosen = jnp.broadcast_to(segment[:, start : start + 128], (8, 128))
        piece = jnp.zeros((8, 128), f32)
        for number, source in enumerate(sources):
            piece = jnp.where(chosen == number, jnp.take_along_axis(source, lane, axis=1), piece)
        pieces.append(piece)
    x = jnp.concatenate(pieces, axis=1)
    column = x.T
    for c in range(3):
        down_ref[c] = jnp.broadcast_to(column[:, c : c + 1], (POINTS, 128))
    edge = boundary.astype(f32) - 0.5

    def fill(row_start, row_stop, col_start, col_stop):
        group = 128
        width = col_stop - col_start
        across = [x[c : c + 1, col_start:col_stop] for c in range(3)]
        col_ids = col_start + lax.broadcasted_iota(jnp.int32, (1, width), 1)
        col_side = col_ids.astype(f32) - edge

        def widen(block):
            return jnp.concatenate([block] * (width // 128), axis=1)

        @pl.loop(0, (row_stop - row_start) // group)
        def _(block):
            start = pl.multiple_of(row_start + block * group, group)
            dist_sq = None
            for c in range(3):
                offset = widen(down_ref[c, pl.ds(start, group), :]) - across[c]
                dist_sq = offset * offset if c == 0 else dist_sq + offset * offset
            root = dist_sq * lax.rsqrt(jnp.maximum(dist_sq, 1e-37))
            scaled = SQRT_THREE * root
            values = (1.0 + scaled) * jnp.exp(-scaled)
            ids = start + lax.broadcasted_iota(jnp.int32, (group, 128), 0)
            same = widen(ids.astype(f32) - edge) * col_side > 0.0
            values = jnp.where(same, values, 0.0)
            values = values + jnp.where(widen(ids) == col_ids, NOISE_VAR, 0.0)
            tile_ref[pl.ds(start, group), col_start:col_stop] = values.astype(bf16)

    tile_ref[:LEAST, MOST:] = jnp.zeros((LEAST, POINTS - MOST), bf16)
    tile_ref[MOST:, :LEAST] = jnp.zeros((POINTS - MOST, LEAST), bf16)
    copies = []
    for number, (start, stop, low, high) in enumerate(
        ((0, LEAST, 0, MOST), (LEAST, MOST, 0, POINTS), (MOST, POINTS, LEAST, POINTS))
    ):
        fill(start, stop, low, high)
        rows = pl.ds(start, stop - start)
        copies.append(
            pltpu.make_async_copy(tile_ref.at[rows], tile_hbm.at[rows], sems.at[number])
        )
        copies[-1].start()

    v = right_ref[...]
    rounded = v.astype(bf16)
    leaf = dot(rounded, tile_ref[...], NN)
    image, curvature = leaf_level(v, rounded, leaf, boundary, basis_ref, coupling_ref)
    image_ref[...] = image
    scalars_ref[...] = jnp.concatenate(
        [curvature, rows_of(v * v), jnp.zeros((6, PROBES), f32)], axis=0
    )
    for copy in copies:
        copy.wait()


def leaf_kernel(
    sizes_ref, residual_ref, first_image_ref, tile_hbm, basis_ref, coupling_ref,
    image_ref, scalars_ref, tile_ref, sems,
):
    width = POINTS // HALVES
    copies = []
    for half in range(HALVES):
        rows = pl.ds(width * half, width)
        copies.append(pltpu.make_async_copy(tile_hbm.at[rows], tile_ref.at[rows], sems.at[half]))
        copies[-1].start()
    v = residual_ref[...]
    rounded = v.astype(bf16)
    leaf = None
    for half in range(HALVES):
        span = slice(width * half, width * (half + 1))
        copies[half].wait()
        part = dot(rounded[:, span], tile_ref[span, :], NN)
        leaf = part if half == 0 else leaf + part
    image, curvature = leaf_level(
        v, rounded, leaf, sizes_ref[0, 0], basis_ref, coupling_ref
    )
    image_ref[...] = image
    scalars_ref[...] = jnp.concatenate(
        [
            curvature,
            rows_of(v * v),
            rows_of(v * first_image_ref[...]),
            jnp.zeros((5, PROBES), f32),
        ],
        axis=0,
    )


def pair_sums(got_ref):
    sums = [[got_ref[ROWS * d : ROWS * d + 8, :] for d in range(PLANE)]]
    for _ in range(4):
        last = sums[-1]
        sums.append([last[2 * i] + last[2 * i + 1] for i in range(len(last) // 2)])
    return sums


def total(got_ref, count, stride, start, rows):
    parts = [got_ref[stride * d + start : stride * d + start + rows, :] for d in range(count)]
    while len(parts) > 1:
        parts = [parts[2 * i] + parts[2 * i + 1] for i in range(len(parts) // 2)]
    return parts[0]


def squares(nodes):
    result = nodes[0] * nodes[0]
    for node in nodes[1:]:
        result = result + node * node
    return result


def plane_kernel(got_ref, scalars_ref, send_ref):
    ids = row_ids(8)
    sums = pair_sums(got_ref)
    square = jnp.zeros((8, PROBES), f32)
    for level in range(1, 5):
        square = jnp.where(ids // 2 == level - 1, squares(sums[level]), square)
    fifth = total(got_ref, PLANE, ROWS, 16, 2)
    curvature = jnp.sum(square, axis=0, keepdims=True) + jnp.sum(
        fifth * fifth, axis=0, keepdims=True
    )
    scalars = scalars_ref[0:3, :] + jnp.where(row_ids(3) == 0, curvature, 0.0)
    block = jnp.concatenate([total(got_ref, PLANE, ROWS, 8, 8), scalars], axis=0)
    for z in range(DEPTH):
        send_ref[Z_ROWS * z : Z_ROWS * (z + 1), :] = block


def depth_kernel(got_ref, z_got_ref, send_ref):
    own = lax.axis_index("pts") // PLANE
    ids = row_ids(8)
    reach = jnp.left_shift(2, ids // 2)
    pair = jnp.zeros((8, PROBES), f32)
    nodes = []
    for z in range(DEPTH):
        block = z_got_ref[Z_ROWS * z : Z_ROWS * z + 8, :]
        nodes.append(block)
        apart = jnp.bitwise_xor(own, z)
        pair = pair + jnp.where(apart < reach, block, 0.0)
    square = jnp.zeros((8, PROBES), f32)
    for level in range(4):
        nodes = [nodes[2 * i] + nodes[2 * i + 1] for i in range(len(nodes) // 2)]
        square = jnp.where(ids // 2 == level, squares(nodes), square)
    curvature = jnp.sum(square, axis=0, keepdims=True)
    scalars = total(z_got_ref, DEPTH, Z_ROWS, 8, 3)
    scalars = scalars + jnp.where(row_ids(3) == 0, curvature, 0.0)
    tail = jnp.concatenate([pair, total(got_ref, PLANE, ROWS, 16, 2), scalars], axis=0)
    sums = pair_sums(got_ref)
    for d in range(PLANE):
        first = sums[4][d >> 4]
        for level in (3, 2, 1):
            first = jnp.where(ids // 2 == level - 1, sums[level][d >> level], first)
        send_ref[BACK * d : BACK * d + 8, :] = first
        send_ref[BACK * d + 8 : BACK * (d + 1), :] = tail


def level_coefficients(got_ref, coupling_ref):
    coefficients = []
    for level in range(1, 10):
        mixed = jnp.concatenate(
            [
                got_ref[pl.ds(first_row(level) + half, PLANE, stride=BACK), :]
                for half in range(2)
            ],
            axis=0,
        )
        coefficients.append(dot_split(coupling_ref[0, level, :RANK, :], mixed, NN))
    return jnp.concatenate(coefficients, axis=0).astype(bf16)


def expand(coefficients, basis_ref, span):
    width = span.stop - span.start
    return dot(coefficients, basis_ref[1:10, :, span].reshape(9 * RANK, width), TN)


def turn_kernel(
    got_ref, right_ref, image_ref, basis_ref, coupling_ref,
    residual_ref, whole_image_ref, send_hbm, keep_ref, send_ref, sem,
):
    scalars = total(got_ref, PLANE, BACK, 18, 3)
    curvature, norm = scalars[0:1], scalars[1:2]
    step = norm / curvature
    coefficients = level_coefficients(got_ref, coupling_ref)
    whole = image_ref[...] + expand(coefficients, basis_ref, slice(0, POINTS))
    residual = right_ref[...] - down_rows(step) * whole
    whole_image_ref[...] = whole
    residual_ref[...] = residual
    keep_ref[...] = jnp.concatenate(
        [step, curvature, norm, jnp.zeros((5, PROBES), f32)], axis=0
    )
    wide = basis_ref[1:10].reshape(9 * RANK, POINTS)
    send_levels(dot(wide, residual.astype(bf16), NT), coupling_ref, send_ref)
    out = pltpu.make_async_copy(send_ref, send_hbm, sem.at[0])
    out.start()
    out.wait()


def end_kernel(
    got_ref, right_ref, residual_ref, first_image_ref, image_ref, basis_ref, coupling_ref,
    keep_ref, solution_hbm, last_hbm, solution_ref, last_ref, sems,
):
    scalars = total(got_ref, PLANE, BACK, 18, 3)
    own, norm, cross = scalars[0:1], scalars[1:2], scalars[2:3]
    step, curvature, norm_before = keep_ref[0:1, :], keep_ref[1:2, :], keep_ref[2:3, :]
    ratio = norm / norm_before
    step_now = norm / (own + 2.0 * ratio * cross + ratio * ratio * curvature)
    ratio_down, step_down = down_rows(ratio), down_rows(step_now)
    right, residual = right_ref[...], residual_ref[...]
    direction = residual + ratio_down * right
    solution_ref[...] = down_rows(step) * right + step_down * direction
    copies = [pltpu.make_async_copy(solution_ref, solution_hbm, sems.at[HALVES])]
    copies[0].start()
    coefficients = level_coefficients(got_ref, coupling_ref)
    width = POINTS // HALVES
    for half in range(HALVES):
        span = slice(width * half, width * (half + 1))
        image = image_ref[:, span] + expand(coefficients, basis_ref, span)
        image = image + ratio_down[:, span] * first_image_ref[:, span]
        last_ref[:, span] = residual[:, span] - step_down[:, span] * image
        columns = pl.ds(width * half, width)
        copies.append(
            pltpu.make_async_copy(
                last_ref.at[:, columns], last_hbm.at[:, columns], sems.at[half]
            )
        )
        copies[-1].start()
    for copy in copies:
        copy.wait()


VMEM = pl.BlockSpec(memory_space=pltpu.VMEM)
SMEM = pl.BlockSpec(memory_space=pltpu.SMEM)
HBM = pl.BlockSpec(memory_space=pltpu.HBM)


def call(body, outs, ins, megabytes, cost, scratch=(), name=None, far_ins=(), far_outs=()):
    specs = [SMEM if a.dtype == jnp.int32 and a.shape == (1, 2) else VMEM for a in ins]
    for place in far_ins:
        specs[place] = HBM
    return pl.pallas_call(
        body,
        out_shape=[
            (pltpu.HBM if place in far_outs else jax.ShapeDtypeStruct)(shape, kind)
            for place, (shape, kind) in enumerate(outs)
        ],
        in_specs=specs,
        out_specs=[HBM if place in far_outs else VMEM for place in range(len(outs))],
        scratch_shapes=list(scratch),
        compiler_params=pltpu.CompilerParams(vmem_limit_bytes=megabytes << 20),
        cost_estimate=pl.CostEstimate(flops=cost, bytes_accessed=2 << 20, transcendentals=0),
        name=name,
    )(*ins)


def plane_groups(count):
    return [list(range(PLANE * z, PLANE * (z + 1))) for z in range(count // PLANE)]


def depth_groups(count):
    return [list(range(place, count, PLANE)) for place in range(PLANE)]


def exchange(rows, groups):
    members = len(groups[0])
    blocks = rows.reshape(members, 1, rows.shape[0] // members * PROBES)
    got = lax.all_to_all(blocks, "pts", 0, 0, axis_index_groups=groups)
    return got.reshape(rows.shape)


def on_device(right_side, coordinates, tree_order, leaf_sizes, level_basis, coupling):
    count = lax.axis_size("pts")
    planes, depths = plane_groups(count), depth_groups(count)
    field = ((PROBES, POINTS), f32)
    message = ((PLANE * ROWS, PROBES), f32)
    back_message = ((PLANE * BACK, PROBES), f32)
    z_message = ((DEPTH * Z_ROWS, PROBES), f32)
    row_block = ((8, PROBES), f32)
    message_scratch = pltpu.VMEM(*message)

    def tree(send, scalars_of):
        got = exchange(send, planes)
        local = scalars_of()
        (z_send,) = call(plane_kernel, [z_message], [got, local[-1]], 2, 1 << 20, name="plane")
        z_got = exchange(z_send, depths)
        (back,) = call(depth_kernel, [back_message], [got, z_got], 2, 1 << 20, name="depth")
        return local, exchange(back, planes)

    (send,) = call(
        start_kernel,
        [message],
        [right_side, level_basis, coupling],
        60,
        1 << 26,
        scratch=[
            pltpu.VMEM(right_side.shape, f32),
            pltpu.VMEM((9, RANK, POINTS), bf16),
            pltpu.VMEM(coupling.shape, f32),
            message_scratch,
            pltpu.SemaphoreType.DMA((2 * HALVES + 2,)),
        ],
        name="start",
        far_ins=(0, 1, 2),
        far_outs=(0,),
    )
    (tile, image, _), got = tree(
        send,
        lambda: call(
            tile_kernel,
            [((POINTS, POINTS), bf16), field, row_block],
            [coordinates, tree_order, leaf_sizes, right_side, level_basis, coupling],
            12,
            4 << 30,
            scratch=[
                pltpu.VMEM((POINTS, POINTS), bf16),
                pltpu.VMEM((3, POINTS, 128), f32),
                pltpu.SemaphoreType.DMA((3,)),
            ],
            name="tile",
            far_outs=(0,),
        ),
    )
    residual, first_image, send, keep = call(
        turn_kernel,
        [field, field, message, row_block],
        [got, right_side, image, level_basis, coupling],
        8,
        1 << 28,
        scratch=[message_scratch, pltpu.SemaphoreType.DMA((1,))],
        name="turn",
        far_outs=(2,),
    )
    (image, _), got = tree(
        send,
        lambda: call(
            leaf_kernel,
            [field, row_block],
            [leaf_sizes, residual, first_image, tile, level_basis, coupling],
            8,
            1 << 30,
            scratch=[
                pltpu.VMEM((POINTS, POINTS), bf16),
                pltpu.SemaphoreType.DMA((HALVES,)),
            ],
            name="leaf",
            far_ins=(3,),
        ),
    )
    return tuple(
        call(
            end_kernel,
            [field, field],
            [got, right_side, residual, first_image, image, level_basis, coupling, keep],
            8,
            1 << 28,
            scratch=[
                pltpu.VMEM(*field),
                pltpu.VMEM(*field),
                pltpu.SemaphoreType.DMA((HALVES + 1,)),
            ],
            name="end",
            far_outs=(0, 1),
        )
    )


def solution(mesh):
    in_specs = (
        P(None, "pts"),
        P(None, "pts"),
        P("pts", None),
        P("pts", None),
        P(None, None, "pts"),
        P("pts", None, None, None),
    )
    out_specs = (P(None, "pts"), P(None, "pts"))
    return jax.shard_map(
        on_device, mesh=mesh, in_specs=in_specs, out_specs=out_specs, check_vma=False
    )
```

```python
import functools

import jax
import jax.numpy as jnp
from jax import lax
from jax.experimental import pallas as pl
from jax.experimental.pallas import tpu as pltpu
from jax.sharding import PartitionSpec as P

f32 = jnp.float32
bf16 = jnp.bfloat16

SQRT_THREE = 1.7320508075688772
NOISE_VAR = 1.0

RANK = 32
PROBES = 128
POINTS = 1024
PLANE = 32
DEPTH = 16
ROWS = 18
Z_ROWS = 8
LEAST = 384
MOST = 640
HALVES = 2

NT = (((1,), (1,)), ((), ()))
TN = (((0,), (0,)), ((), ()))
NN = (((1,), (0,)), ((), ()))


def first_row(level):
    if level < 5:
        return 2 * (level - 1)
    return 16 if level == 5 else 8 + 2 * (level - 6)


def dot(a, b, dims):
    return lax.dot_general(a, b, dims, preferred_element_type=f32)


def halves(x):
    high = x.astype(bf16)
    return high, (x - high.astype(f32)).astype(bf16)


def dot_split(a, b, dims):
    a_high, a_low = halves(a)
    b_high, b_low = halves(b)
    a_dim, b_dim = dims[0][0][0], dims[0][1][0]
    return dot(
        jnp.concatenate([a_high, a_high, a_low], axis=a_dim),
        jnp.concatenate([b_high, b_low, b_high], axis=b_dim),
        dims,
    )


def rows_of(products):
    part = products[:, :PROBES]
    for start in range(PROBES, POINTS, PROBES):
        part = part + products[:, start : start + PROBES]
    return jnp.sum(part.T, axis=0, keepdims=True)


def down_rows(row):
    square = jnp.broadcast_to(row, (PROBES, PROBES)).T
    return jnp.concatenate([square] * (POINTS // PROBES), axis=1)


def row_ids(rows):
    return lax.broadcasted_iota(jnp.int32, (rows, PROBES), 0)


def send_levels(projected, coupling_ref, send_ref):
    for level in range(1, 10):
        own = coupling_ref[0, level, :RANK, :]
        partial = dot_split(own, projected[RANK * (level - 1) : RANK * level], TN)
        for half in range(2):
            send_ref[pl.ds(first_row(level) + half, PLANE, stride=ROWS), :] = partial[
                PLANE * half : PLANE * (half + 1)
            ]


def start_kernel(
    right_hbm, basis_hbm, coupling_hbm, send_hbm,
    right_ref, basis_ref, coupling_ref, send_ref, sems,
):
    width = POINTS // HALVES
    fetches = []
    for half in range(HALVES):
        span = pl.ds(width * half, width)
        right_copy = pltpu.make_async_copy(
            right_hbm.at[:, span], right_ref.at[:, span], sems.at[2 * half]
        )
        basis_copy = pltpu.make_async_copy(
            basis_hbm.at[pl.ds(1, 9), :, span],
            basis_ref.at[:, :, span],
            sems.at[2 * half + 1],
        )
        right_copy.start()
        basis_copy.start()
        fetches.append((right_copy, basis_copy))
    factors = pltpu.make_async_copy(coupling_hbm, coupling_ref, sems.at[2 * HALVES])
    factors.start()
    projected = None
    for half, (right_copy, basis_copy) in enumerate(fetches):
        span = slice(width * half, width * (half + 1))
        right_copy.wait()
        basis_copy.wait()
        part = dot(
            basis_ref[:, :, span].reshape(9 * RANK, width),
            right_ref[:, span].astype(bf16),
            NT,
        )
        projected = part if half == 0 else projected + part
    factors.wait()
    send_levels(projected, coupling_ref, send_ref)
    out = pltpu.make_async_copy(send_ref, send_hbm, sems.at[2 * HALVES + 1])
    out.start()
    out.wait()


def leaf_level(v, rounded, leaf, boundary, basis_ref, coupling_ref):
    wide = basis_ref[0].astype(f32)
    in_first = lax.broadcasted_iota(jnp.int32, (RANK, POINTS), 1) < boundary
    both = jnp.concatenate(
        [jnp.where(in_first, wide, 0.0), jnp.where(in_first, 0.0, wide)], axis=0
    ).astype(bf16)
    factor = coupling_ref[0, 0]
    mixed = dot_split(factor, dot(both, rounded, NT), TN)
    coefficients = dot_split(factor, mixed, NN).astype(bf16)
    image = leaf + dot(coefficients, both, TN)
    curvature = rows_of(v * leaf) + jnp.sum(mixed * mixed, axis=0, keepdims=True)
    return image, curvature


def tile_kernel(
    coordinates_ref, order_ref, sizes_ref, right_ref, basis_ref, coupling_ref,
    tile_hbm, image_ref, scalars_ref, tile_ref, down_ref, sems,
):
    boundary = sizes_ref[0, 0]
    order = order_ref[...]
    place, segment = jnp.bitwise_and(order, 127), jnp.right_shift(order, 7)
    sources = [
        jnp.concatenate(
            [coordinates_ref[:, start : start + 128], jnp.zeros((5, 128), f32)], axis=0
        )
        for start in range(0, POINTS, 128)
    ]
    pieces = []
    for start in range(0, POINTS, 128):
        lane = jnp.broadcast_to(place[:, start : start + 128], (8, 128))
        chosen = jnp.broadcast_to(segment[:, start : start + 128], (8, 128))
        piece = jnp.zeros((8, 128), f32)
        for number, source in enumerate(sources):
            piece = jnp.where(chosen == number, jnp.take_along_axis(source, lane, axis=1), piece)
        pieces.append(piece)
    x = jnp.concatenate(pieces, axis=1)
    column = x.T
    for c in range(3):
        down_ref[c] = jnp.broadcast_to(column[:, c : c + 1], (POINTS, 128))
    edge = boundary.astype(f32) - 0.5

    def fill(row_start, row_stop, col_start, col_stop):
        group = 128
        width = col_stop - col_start
        across = [x[c : c + 1, col_start:col_stop] for c in range(3)]
        col_ids = col_start + lax.broadcasted_iota(jnp.int32, (1, width), 1)
        col_side = col_ids.astype(f32) - edge

        def widen(block):
            return jnp.concatenate([block] * (width // 128), axis=1)

        @pl.loop(0, (row_stop - row_start) // group)
        def _(block):
            start = pl.multiple_of(row_start + block * group, group)
            dist_sq = None
            for c in range(3):
                offset = widen(down_ref[c, pl.ds(start, group), :]) - across[c]
                dist_sq = offset * offset if c == 0 else dist_sq + offset * offset
            root = dist_sq * lax.rsqrt(jnp.maximum(dist_sq, 1e-37))
            scaled = SQRT_THREE * root
            values = (1.0 + scaled) * jnp.exp(-scaled)
            ids = start + lax.broadcasted_iota(jnp.int32, (group, 128), 0)
            same = widen(ids.astype(f32) - edge) * col_side > 0.0
            values = jnp.where(same, values, 0.0)
            values = values + jnp.where(widen(ids) == col_ids, NOISE_VAR, 0.0)
            tile_ref[pl.ds(start, group), col_start:col_stop] = values.astype(bf16)

    tile_ref[:LEAST, MOST:] = jnp.zeros((LEAST, POINTS - MOST), bf16)
    tile_ref[MOST:, :LEAST] = jnp.zeros((POINTS - MOST, LEAST), bf16)
    copies = []
    for number, (start, stop, low, high) in enumerate(
        ((0, LEAST, 0, MOST), (LEAST, MOST, 0, POINTS), (MOST, POINTS, LEAST, POINTS))
    ):
        fill(start, stop, low, high)
        rows = pl.ds(start, stop - start)
        copies.append(
            pltpu.make_async_copy(tile_ref.at[rows], tile_hbm.at[rows], sems.at[number])
        )
        copies[-1].start()

    v = right_ref[...]
    rounded = v.astype(bf16)
    leaf = dot(rounded, tile_ref[...], NN)
    image, curvature = leaf_level(v, rounded, leaf, boundary, basis_ref, coupling_ref)
    image_ref[...] = image
    scalars_ref[0:1, :] = curvature
    scalars_ref[1:2, :] = rows_of(v * v)
    for copy in copies:
        copy.wait()


def pair_sums(got_ref):
    sums = [[got_ref[ROWS * d : ROWS * d + 8, :] for d in range(PLANE)]]
    for _ in range(4):
        last = sums[-1]
        sums.append([last[2 * i] + last[2 * i + 1] for i in range(len(last) // 2)])
    return sums


def total(got_ref, count, stride, start, rows):
    parts = [got_ref[stride * d + start : stride * d + start + rows, :] for d in range(count)]
    while len(parts) > 1:
        parts = [parts[2 * i] + parts[2 * i + 1] for i in range(len(parts) // 2)]
    return parts[0]


def squares(nodes):
    result = nodes[0] * nodes[0]
    for node in nodes[1:]:
        result = result + node * node
    return result


def plane_kernel(count, got_ref, scalars_ref, send_ref):
    ids = row_ids(8)
    sums = pair_sums(got_ref)
    square = jnp.zeros((8, PROBES), f32)
    for level in range(1, 5):
        square = jnp.where(ids // 2 == level - 1, squares(sums[level]), square)
    fifth = total(got_ref, PLANE, ROWS, 16, 2)
    curvature = jnp.sum(square, axis=0, keepdims=True) + jnp.sum(
        fifth * fifth, axis=0, keepdims=True
    )
    scalars = scalars_ref[...] + jnp.where(row_ids(count) == 0, curvature, 0.0)
    block = jnp.concatenate([total(got_ref, PLANE, ROWS, 8, 8), scalars], axis=0)
    stride = Z_ROWS + count
    for z in range(DEPTH):
        send_ref[stride * z : stride * (z + 1), :] = block


def depth_kernel(count, got_ref, z_got_ref, send_ref):
    z_stride, stride = Z_ROWS + count, ROWS + count
    own = lax.axis_index("pts") // PLANE
    ids = row_ids(8)
    reach = jnp.left_shift(2, ids // 2)
    pair = jnp.zeros((8, PROBES), f32)
    nodes = []
    for z in range(DEPTH):
        block = z_got_ref[z_stride * z : z_stride * z + 8, :]
        nodes.append(block)
        apart = jnp.bitwise_xor(own, z)
        pair = pair + jnp.where(apart < reach, block, 0.0)
    square = jnp.zeros((8, PROBES), f32)
    for level in range(4):
        nodes = [nodes[2 * i] + nodes[2 * i + 1] for i in range(len(nodes) // 2)]
        square = jnp.where(ids // 2 == level, squares(nodes), square)
    curvature = jnp.sum(square, axis=0, keepdims=True)
    scalars = total(z_got_ref, DEPTH, z_stride, 8, count)
    scalars = scalars + jnp.where(row_ids(count) == 0, curvature, 0.0)
    tail = jnp.concatenate([pair, total(got_ref, PLANE, ROWS, 16, 2), scalars], axis=0)
    sums = pair_sums(got_ref)
    for d in range(PLANE):
        first = sums[4][d >> 4]
        for level in (3, 2, 1):
            first = jnp.where(ids // 2 == level - 1, sums[level][d >> level], first)
        send_ref[stride * d : stride * d + 8, :] = first
        send_ref[stride * d + 8 : stride * (d + 1), :] = tail


def level_coefficients(got_ref, coupling_ref, stride):
    coefficients = []
    for level in range(1, 10):
        mixed = jnp.concatenate(
            [
                got_ref[pl.ds(first_row(level) + half, PLANE, stride=stride), :]
                for half in range(2)
            ],
            axis=0,
        )
        coefficients.append(dot_split(coupling_ref[0, level, :RANK, :], mixed, NN))
    return jnp.concatenate(coefficients, axis=0).astype(bf16)


def expand(coefficients, basis_ref, span):
    width = span.stop - span.start
    return dot(coefficients, basis_ref[1:10, :, span].reshape(9 * RANK, width), TN)


def turn_kernel(
    sizes_ref, got_ref, right_ref, image_ref, tile_ref, basis_ref, coupling_ref,
    residual_ref, whole_image_ref, next_image_ref, scalars_ref, send_ref, keep_ref,
):
    scalars = total(got_ref, PLANE, ROWS + 2, ROWS, 2)
    curvature, norm = scalars[0:1], scalars[1:2]
    step = norm / curvature
    coefficients = level_coefficients(got_ref, coupling_ref, ROWS + 2)
    whole = image_ref[...] + expand(coefficients, basis_ref, slice(0, POINTS))
    residual = right_ref[...] - down_rows(step) * whole
    whole_image_ref[...] = whole
    residual_ref[...] = residual
    keep_ref[0:1, :] = step
    keep_ref[1:2, :] = curvature
    keep_ref[2:3, :] = norm
    rounded = residual.astype(bf16)
    wide = basis_ref[1:10].reshape(9 * RANK, POINTS)
    send_levels(dot(wide, rounded, NT), coupling_ref, send_ref)
    leaf = dot(rounded, tile_ref[...], NN)
    image, own = leaf_level(residual, rounded, leaf, sizes_ref[0, 0], basis_ref, coupling_ref)
    next_image_ref[...] = image
    scalars_ref[0:1, :] = own
    scalars_ref[1:2, :] = rows_of(residual * residual)
    scalars_ref[2:3, :] = rows_of(residual * whole)


def end_kernel(
    got_ref, right_ref, residual_ref, first_image_ref, image_ref, basis_ref, coupling_ref,
    keep_ref, solution_hbm, last_hbm, solution_ref, last_ref, sems,
):
    scalars = total(got_ref, PLANE, ROWS + 3, ROWS, 3)
    own, norm, cross = scalars[0:1], scalars[1:2], scalars[2:3]
    step, curvature, norm_before = keep_ref[0:1, :], keep_ref[1:2, :], keep_ref[2:3, :]
    ratio = norm / norm_before
    step_now = norm / (own + 2.0 * ratio * cross + ratio * ratio * curvature)
    ratio_down, step_down = down_rows(ratio), down_rows(step_now)
    right, residual = right_ref[...], residual_ref[...]
    direction = residual + ratio_down * right
    solution_ref[...] = down_rows(step) * right + step_down * direction
    copies = [pltpu.make_async_copy(solution_ref, solution_hbm, sems.at[HALVES])]
    copies[0].start()
    coefficients = level_coefficients(got_ref, coupling_ref, ROWS + 3)
    width = POINTS // HALVES
    for half in range(HALVES):
        span = slice(width * half, width * (half + 1))
        image = image_ref[:, span] + expand(coefficients, basis_ref, span)
        image = image + ratio_down[:, span] * first_image_ref[:, span]
        last_ref[:, span] = residual[:, span] - step_down[:, span] * image
        columns = pl.ds(width * half, width)
        copies.append(
            pltpu.make_async_copy(
                last_ref.at[:, columns], last_hbm.at[:, columns], sems.at[half]
            )
        )
        copies[-1].start()
    for copy in copies:
        copy.wait()


VMEM = pl.BlockSpec(memory_space=pltpu.VMEM)
SMEM = pl.BlockSpec(memory_space=pltpu.SMEM)
HBM = pl.BlockSpec(memory_space=pltpu.HBM)


def call(body, outs, ins, megabytes, cost, scratch=(), name=None, far_ins=(), far_outs=()):
    specs = [SMEM if a.dtype == jnp.int32 and a.shape == (1, 2) else VMEM for a in ins]
    for place in far_ins:
        specs[place] = HBM
    return pl.pallas_call(
        body,
        out_shape=[
            (pltpu.HBM if place in far_outs else jax.ShapeDtypeStruct)(shape, kind)
            for place, (shape, kind) in enumerate(outs)
        ],
        in_specs=specs,
        out_specs=[HBM if place in far_outs else VMEM for place in range(len(outs))],
        scratch_shapes=list(scratch),
        compiler_params=pltpu.CompilerParams(vmem_limit_bytes=megabytes << 20),
        cost_estimate=pl.CostEstimate(flops=cost, bytes_accessed=2 << 20, transcendentals=0),
        name=name,
    )(*ins)


def plane_groups(count):
    return [list(range(PLANE * z, PLANE * (z + 1))) for z in range(count // PLANE)]


def depth_groups(count):
    return [list(range(place, count, PLANE)) for place in range(PLANE)]


def exchange(rows, groups):
    members = len(groups[0])
    blocks = rows.reshape(members, 1, rows.shape[0] // members * PROBES)
    got = lax.all_to_all(blocks, "pts", 0, 0, axis_index_groups=groups)
    return got.reshape(rows.shape)


def on_device(right_side, coordinates, tree_order, leaf_sizes, level_basis, coupling):
    count = lax.axis_size("pts")
    planes, depths = plane_groups(count), depth_groups(count)
    field = ((PROBES, POINTS), f32)
    message = ((PLANE * ROWS, PROBES), f32)
    message_scratch = pltpu.VMEM(*message)

    def scalar_rows(rows):
        return ((rows, PROBES), f32)

    def tree(send, scalars_of, rows):
        got = exchange(send, planes)
        local = scalars_of()
        (z_send,) = call(
            functools.partial(plane_kernel, rows),
            [((DEPTH * (Z_ROWS + rows), PROBES), f32)],
            [got, local[-1]],
            2,
            1 << 20,
            name="plane",
        )
        z_got = exchange(z_send, depths)
        (back,) = call(
            functools.partial(depth_kernel, rows),
            [((PLANE * (ROWS + rows), PROBES), f32)],
            [got, z_got],
            2,
            1 << 20,
            name="depth",
        )
        return local, exchange(back, planes)

    (send,) = call(
        start_kernel,
        [message],
        [right_side, level_basis, coupling],
        60,
        1 << 26,
        scratch=[
            pltpu.VMEM(right_side.shape, f32),
            pltpu.VMEM((9, RANK, POINTS), bf16),
            pltpu.VMEM(coupling.shape, f32),
            message_scratch,
            pltpu.SemaphoreType.DMA((2 * HALVES + 2,)),
        ],
        name="start",
        far_ins=(0, 1, 2),
        far_outs=(0,),
    )
    (tile, image, _), got = tree(
        send,
        lambda: call(
            tile_kernel,
            [((POINTS, POINTS), bf16), field, scalar_rows(2)],
            [coordinates, tree_order, leaf_sizes, right_side, level_basis, coupling],
            12,
            4 << 30,
            scratch=[
                pltpu.VMEM((POINTS, POINTS), bf16),
                pltpu.VMEM((3, POINTS, 128), f32),
                pltpu.SemaphoreType.DMA((3,)),
            ],
            name="tile",
            far_outs=(0,),
        ),
        2,
    )
    residual, first_image, image, scalars, send, keep = call(
        turn_kernel,
        [field, field, field, scalar_rows(3), message, scalar_rows(3)],
        [leaf_sizes, got, right_side, image, tile, level_basis, coupling],
        8,
        1 << 28,
        name="turn",
    )
    _, got = tree(send, lambda: (scalars,), 3)
    return tuple(
        call(
            end_kernel,
            [field, field],
            [got, right_side, residual, first_image, image, level_basis, coupling, keep],
            8,
            1 << 28,
            scratch=[
                pltpu.VMEM(*field),
                pltpu.VMEM(*field),
                pltpu.SemaphoreType.DMA((HALVES + 1,)),
            ],
            name="end",
            far_outs=(0, 1),
        )
    )


def solution(mesh):
    in_specs = (
        P(None, "pts"),
        P(None, "pts"),
        P("pts", None),
        P("pts", None),
        P(None, None, "pts"),
        P("pts", None, None, None),
    )
    out_specs = (P(None, "pts"), P(None, "pts"))
    return jax.shard_map(
        on_device, mesh=mesh, in_specs=in_specs, out_specs=out_specs, check_vma=False
    )
```

```python
import functools

import jax
import jax.numpy as jnp
from jax import lax
from jax.experimental import pallas as pl
from jax.experimental.pallas import tpu as pltpu
from jax.sharding import PartitionSpec as P

f32 = jnp.float32
bf16 = jnp.bfloat16

SQRT_THREE = 1.7320508075688772
NOISE_VAR = 1.0

RANK = 32
PROBES = 128
POINTS = 1024
PLANE = 32
DEPTH = 16
ROWS = 18
Z_ROWS = 8
LEAST = 384
MOST = 640
HALVES = 2

NT = (((1,), (1,)), ((), ()))
TN = (((0,), (0,)), ((), ()))
NN = (((1,), (0,)), ((), ()))


def first_row(level):
    if level < 5:
        return 2 * (level - 1)
    return 16 if level == 5 else 8 + 2 * (level - 6)


def dot(a, b, dims):
    return lax.dot_general(a, b, dims, preferred_element_type=f32)


def halves(x):
    high = x.astype(bf16)
    return high, (x - high.astype(f32)).astype(bf16)


def dot_split(a, b, dims):
    a_high, a_low = halves(a)
    b_high, b_low = halves(b)
    a_dim, b_dim = dims[0][0][0], dims[0][1][0]
    return dot(
        jnp.concatenate([a_high, a_high, a_low], axis=a_dim),
        jnp.concatenate([b_high, b_low, b_high], axis=b_dim),
        dims,
    )


def project_split(wide, v):
    high, low = halves(v)
    return dot(wide, high, NT) + dot(wide, low, NT)


def rows_of(products):
    part = products[:, :PROBES]
    for start in range(PROBES, POINTS, PROBES):
        part = part + products[:, start : start + PROBES]
    return jnp.sum(part.T, axis=0, keepdims=True)


def down_rows(row):
    square = jnp.broadcast_to(row, (PROBES, PROBES)).T
    return jnp.concatenate([square] * (POINTS // PROBES), axis=1)


def row_ids(rows):
    return lax.broadcasted_iota(jnp.int32, (rows, PROBES), 0)


def send_levels(projected, coupling_ref, send_ref):
    for level in range(1, 10):
        own = coupling_ref[0, level, :RANK, :]
        partial = dot_split(own, projected[RANK * (level - 1) : RANK * level], TN)
        for half in range(2):
            send_ref[pl.ds(first_row(level) + half, PLANE, stride=ROWS), :] = partial[
                PLANE * half : PLANE * (half + 1)
            ]


def start_kernel(
    right_hbm, basis_hbm, coupling_hbm, send_hbm,
    right_ref, basis_ref, coupling_ref, send_ref, sems,
):
    width = POINTS // HALVES
    fetches = []
    for half in range(HALVES):
        span = pl.ds(width * half, width)
        right_copy = pltpu.make_async_copy(
            right_hbm.at[:, span], right_ref.at[:, span], sems.at[2 * half]
        )
        basis_copy = pltpu.make_async_copy(
            basis_hbm.at[pl.ds(1, 9), :, span],
            basis_ref.at[:, :, span],
            sems.at[2 * half + 1],
        )
        right_copy.start()
        basis_copy.start()
        fetches.append((right_copy, basis_copy))
    factors = pltpu.make_async_copy(coupling_hbm, coupling_ref, sems.at[2 * HALVES])
    factors.start()
    projected = None
    for half, (right_copy, basis_copy) in enumerate(fetches):
        span = slice(width * half, width * (half + 1))
        right_copy.wait()
        basis_copy.wait()
        part = dot(
            basis_ref[:, :, span].reshape(9 * RANK, width),
            right_ref[:, span].astype(bf16),
            NT,
        )
        projected = part if half == 0 else projected + part
    factors.wait()
    send_levels(projected, coupling_ref, send_ref)
    out = pltpu.make_async_copy(send_ref, send_hbm, sems.at[2 * HALVES + 1])
    out.start()
    out.wait()


def leaf_level(v, rounded, leaf, boundary, basis_ref, coupling_ref):
    wide = basis_ref[0].astype(f32)
    in_first = lax.broadcasted_iota(jnp.int32, (RANK, POINTS), 1) < boundary
    both = jnp.concatenate(
        [jnp.where(in_first, wide, 0.0), jnp.where(in_first, 0.0, wide)], axis=0
    ).astype(bf16)
    factor = coupling_ref[0, 0]
    mixed = dot_split(factor, dot(both, rounded, NT), TN)
    coefficients = dot_split(factor, mixed, NN).astype(bf16)
    image = leaf + dot(coefficients, both, TN)
    curvature = rows_of(v * leaf) + jnp.sum(mixed * mixed, axis=0, keepdims=True)
    return image, curvature


def tile_kernel(
    coordinates_ref, order_ref, sizes_ref, right_ref, basis_ref, coupling_ref,
    tile_hbm, image_ref, parts_ref, scalars_ref,
    tile_ref, down_ref, sems,
):
    boundary = sizes_ref[0, 0]
    order = order_ref[...]
    place, segment = jnp.bitwise_and(order, 127), jnp.right_shift(order, 7)
    sources = [
        jnp.concatenate(
            [coordinates_ref[:, start : start + 128], jnp.zeros((5, 128), f32)], axis=0
        )
        for start in range(0, POINTS, 128)
    ]
    pieces = []
    for start in range(0, POINTS, 128):
        lane = jnp.broadcast_to(place[:, start : start + 128], (8, 128))
        chosen = jnp.broadcast_to(segment[:, start : start + 128], (8, 128))
        piece = jnp.zeros((8, 128), f32)
        for number, source in enumerate(sources):
            piece = jnp.where(chosen == number, jnp.take_along_axis(source, lane, axis=1), piece)
        pieces.append(piece)
    x = jnp.concatenate(pieces, axis=1)
    column = x.T
    for c in range(3):
        down_ref[c] = jnp.broadcast_to(column[:, c : c + 1], (POINTS, 128))
    edge = boundary.astype(f32) - 0.5

    def fill(row_start, row_stop, col_start, col_stop):
        group = 128
        width = col_stop - col_start
        across = [x[c : c + 1, col_start:col_stop] for c in range(3)]
        col_ids = col_start + lax.broadcasted_iota(jnp.int32, (1, width), 1)
        col_side = col_ids.astype(f32) - edge

        def widen(block):
            return jnp.concatenate([block] * (width // 128), axis=1)

        @pl.loop(0, (row_stop - row_start) // group)
        def _(block):
            start = pl.multiple_of(row_start + block * group, group)
            dist_sq = None
            for c in range(3):
                offset = widen(down_ref[c, pl.ds(start, group), :]) - across[c]
                dist_sq = offset * offset if c == 0 else dist_sq + offset * offset
            root = dist_sq * lax.rsqrt(jnp.maximum(dist_sq, 1e-37))
            scaled = SQRT_THREE * root
            values = (1.0 + scaled) * jnp.exp(-scaled)
            ids = start + lax.broadcasted_iota(jnp.int32, (group, 128), 0)
            same = widen(ids.astype(f32) - edge) * col_side > 0.0
            values = jnp.where(same, values, 0.0)
            values = values + jnp.where(widen(ids) == col_ids, NOISE_VAR, 0.0)
            tile_ref[pl.ds(start, group), col_start:col_stop] = values.astype(bf16)

    tile_ref[:LEAST, MOST:] = jnp.zeros((LEAST, POINTS - MOST), bf16)
    tile_ref[MOST:, :LEAST] = jnp.zeros((POINTS - MOST, LEAST), bf16)
    copies = []
    for number, (start, stop, low, high) in enumerate(
        ((0, LEAST, 0, MOST), (LEAST, MOST, 0, POINTS), (MOST, POINTS, LEAST, POINTS))
    ):
        fill(start, stop, low, high)
        rows = pl.ds(start, stop - start)
        copies.append(
            pltpu.make_async_copy(tile_ref.at[rows], tile_hbm.at[rows], sems.at[number])
        )
        copies[-1].start()

    v = right_ref[...]
    rounded = v.astype(bf16)
    leaf = dot(rounded, tile_ref[...], NN)
    image, curvature = leaf_level(v, rounded, leaf, boundary, basis_ref, coupling_ref)
    image_ref[...] = image
    scalars_ref[0:1, :] = curvature
    scalars_ref[1:2, :] = rows_of(v * v)
    wide = basis_ref[1:10].reshape(9 * RANK, POINTS)
    parts_ref[:, :PROBES] = project_split(wide, v)
    parts_ref[:, PROBES : 2 * PROBES] = project_split(wide, image)
    parts_ref[:, 2 * PROBES :] = dot(wide, wide, NT)
    for copy in copies:
        copy.wait()


def leaf_kernel(
    sizes_ref, residual_ref, first_image_ref, tile_hbm, basis_ref, coupling_ref,
    image_ref, scalars_ref, tile_ref, sems,
):
    width = POINTS // HALVES
    copies = []
    for half in range(HALVES):
        rows = pl.ds(width * half, width)
        copies.append(pltpu.make_async_copy(tile_hbm.at[rows], tile_ref.at[rows], sems.at[half]))
        copies[-1].start()
    v = residual_ref[...]
    rounded = v.astype(bf16)
    leaf = None
    for half in range(HALVES):
        span = slice(width * half, width * (half + 1))
        copies[half].wait()
        part = dot(rounded[:, span], tile_ref[span, :], NN)
        leaf = part if half == 0 else leaf + part
    image, curvature = leaf_level(
        v, rounded, leaf, sizes_ref[0, 0], basis_ref, coupling_ref
    )
    image_ref[...] = image
    scalars_ref[0:1, :] = curvature
    scalars_ref[1:2, :] = rows_of(v * v)
    scalars_ref[2:3, :] = rows_of(v * first_image_ref[...])


def pair_sums(got_ref):
    sums = [[got_ref[ROWS * d : ROWS * d + 8, :] for d in range(PLANE)]]
    for _ in range(4):
        last = sums[-1]
        sums.append([last[2 * i] + last[2 * i + 1] for i in range(len(last) // 2)])
    return sums


def total(got_ref, count, stride, start, rows):
    parts = [got_ref[stride * d + start : stride * d + start + rows, :] for d in range(count)]
    while len(parts) > 1:
        parts = [parts[2 * i] + parts[2 * i + 1] for i in range(len(parts) // 2)]
    return parts[0]


def squares(nodes):
    result = nodes[0] * nodes[0]
    for node in nodes[1:]:
        result = result + node * node
    return result


def plane_kernel(count, got_ref, scalars_ref, send_ref):
    ids = row_ids(8)
    sums = pair_sums(got_ref)
    square = jnp.zeros((8, PROBES), f32)
    for level in range(1, 5):
        square = jnp.where(ids // 2 == level - 1, squares(sums[level]), square)
    fifth = total(got_ref, PLANE, ROWS, 16, 2)
    curvature = jnp.sum(square, axis=0, keepdims=True) + jnp.sum(
        fifth * fifth, axis=0, keepdims=True
    )
    scalars = scalars_ref[...] + jnp.where(row_ids(count) == 0, curvature, 0.0)
    block = jnp.concatenate([total(got_ref, PLANE, ROWS, 8, 8), scalars], axis=0)
    stride = Z_ROWS + count
    for z in range(DEPTH):
        send_ref[stride * z : stride * (z + 1), :] = block


def depth_kernel(count, got_ref, z_got_ref, send_ref):
    z_stride, stride = Z_ROWS + count, ROWS + count
    own = lax.axis_index("pts") // PLANE
    ids = row_ids(8)
    reach = jnp.left_shift(2, ids // 2)
    pair = jnp.zeros((8, PROBES), f32)
    nodes = []
    for z in range(DEPTH):
        block = z_got_ref[z_stride * z : z_stride * z + 8, :]
        nodes.append(block)
        apart = jnp.bitwise_xor(own, z)
        pair = pair + jnp.where(apart < reach, block, 0.0)
    square = jnp.zeros((8, PROBES), f32)
    for level in range(4):
        nodes = [nodes[2 * i] + nodes[2 * i + 1] for i in range(len(nodes) // 2)]
        square = jnp.where(ids // 2 == level, squares(nodes), square)
    curvature = jnp.sum(square, axis=0, keepdims=True)
    scalars = total(z_got_ref, DEPTH, z_stride, 8, count)
    scalars = scalars + jnp.where(row_ids(count) == 0, curvature, 0.0)
    tail = jnp.concatenate([pair, total(got_ref, PLANE, ROWS, 16, 2), scalars], axis=0)
    sums = pair_sums(got_ref)
    for d in range(PLANE):
        first = sums[4][d >> 4]
        for level in (3, 2, 1):
            first = jnp.where(ids // 2 == level - 1, sums[level][d >> level], first)
        send_ref[stride * d : stride * d + 8, :] = first
        send_ref[stride * d + 8 : stride * (d + 1), :] = tail


def level_coefficients(got_ref, coupling_ref, stride):
    coefficients = []
    for level in range(1, 10):
        mixed = jnp.concatenate(
            [
                got_ref[pl.ds(first_row(level) + half, PLANE, stride=stride), :]
                for half in range(2)
            ],
            axis=0,
        )
        coefficients.append(dot_split(coupling_ref[0, level, :RANK, :], mixed, NN))
    return jnp.concatenate(coefficients, axis=0).astype(bf16)


def expand(coefficients, basis_ref, span):
    width = span.stop - span.start
    return dot(coefficients, basis_ref[1:10, :, span].reshape(9 * RANK, width), TN)


def turn_kernel(
    got_ref, right_ref, image_ref, parts_ref, basis_ref, coupling_ref,
    residual_ref, whole_image_ref, send_hbm, keep_ref, send_ref, sem,
):
    scalars = total(got_ref, PLANE, ROWS + 2, ROWS, 2)
    curvature, norm = scalars[0:1], scalars[1:2]
    step = norm / curvature
    coefficients = level_coefficients(got_ref, coupling_ref, ROWS + 2)
    gram_high, gram_low = halves(parts_ref[:, 2 * PROBES :])
    spread = dot(gram_high, coefficients, NN) + dot(gram_low, coefficients, NN)
    projected = parts_ref[:, :PROBES] - step * (parts_ref[:, PROBES : 2 * PROBES] + spread)
    send_levels(projected, coupling_ref, send_ref)
    out = pltpu.make_async_copy(send_ref, send_hbm, sem.at[0])
    out.start()
    whole = image_ref[...] + expand(coefficients, basis_ref, slice(0, POINTS))
    whole_image_ref[...] = whole
    residual_ref[...] = right_ref[...] - down_rows(step) * whole
    keep_ref[0:1, :] = step
    keep_ref[1:2, :] = curvature
    keep_ref[2:3, :] = norm
    out.wait()


def end_kernel(
    got_ref, right_ref, residual_ref, first_image_ref, image_ref, basis_ref, coupling_ref,
    keep_ref, solution_hbm, last_hbm, solution_ref, last_ref, sems,
):
    scalars = total(got_ref, PLANE, ROWS + 3, ROWS, 3)
    own, norm, cross = scalars[0:1], scalars[1:2], scalars[2:3]
    step, curvature, norm_before = keep_ref[0:1, :], keep_ref[1:2, :], keep_ref[2:3, :]
    ratio = norm / norm_before
    step_now = norm / (own + 2.0 * ratio * cross + ratio * ratio * curvature)
    ratio_down, step_down = down_rows(ratio), down_rows(step_now)
    right, residual = right_ref[...], residual_ref[...]
    direction = residual + ratio_down * right
    solution_ref[...] = down_rows(step) * right + step_down * direction
    copies = [pltpu.make_async_copy(solution_ref, solution_hbm, sems.at[HALVES])]
    copies[0].start()
    coefficients = level_coefficients(got_ref, coupling_ref, ROWS + 3)
    width = POINTS // HALVES
    for half in range(HALVES):
        span = slice(width * half, width * (half + 1))
        image = image_ref[:, span] + expand(coefficients, basis_ref, span)
        image = image + ratio_down[:, span] * first_image_ref[:, span]
        last_ref[:, span] = residual[:, span] - step_down[:, span] * image
        columns = pl.ds(width * half, width)
        copies.append(
            pltpu.make_async_copy(
                last_ref.at[:, columns], last_hbm.at[:, columns], sems.at[half]
            )
        )
        copies[-1].start()
    for copy in copies:
        copy.wait()


VMEM = pl.BlockSpec(memory_space=pltpu.VMEM)
SMEM = pl.BlockSpec(memory_space=pltpu.SMEM)
HBM = pl.BlockSpec(memory_space=pltpu.HBM)


def call(body, outs, ins, megabytes, cost, scratch=(), name=None, far_ins=(), far_outs=()):
    specs = [SMEM if a.dtype == jnp.int32 and a.shape == (1, 2) else VMEM for a in ins]
    for place in far_ins:
        specs[place] = HBM
    return pl.pallas_call(
        body,
        out_shape=[
            (pltpu.HBM if place in far_outs else jax.ShapeDtypeStruct)(shape, kind)
            for place, (shape, kind) in enumerate(outs)
        ],
        in_specs=specs,
        out_specs=[HBM if place in far_outs else VMEM for place in range(len(outs))],
        scratch_shapes=list(scratch),
        compiler_params=pltpu.CompilerParams(vmem_limit_bytes=megabytes << 20),
        cost_estimate=pl.CostEstimate(flops=cost, bytes_accessed=2 << 20, transcendentals=0),
        name=name,
    )(*ins)


def plane_groups(count):
    return [list(range(PLANE * z, PLANE * (z + 1))) for z in range(count // PLANE)]


def depth_groups(count):
    return [list(range(place, count, PLANE)) for place in range(PLANE)]


def exchange(rows, groups):
    members = len(groups[0])
    blocks = rows.reshape(members, 1, rows.shape[0] // members * PROBES)
    got = lax.all_to_all(blocks, "pts", 0, 0, axis_index_groups=groups)
    return got.reshape(rows.shape)


def on_device(right_side, coordinates, tree_order, leaf_sizes, level_basis, coupling):
    count = lax.axis_size("pts")
    planes, depths = plane_groups(count), depth_groups(count)
    field = ((PROBES, POINTS), f32)
    message = ((PLANE * ROWS, PROBES), f32)
    message_scratch = pltpu.VMEM(*message)
    parts_block = ((9 * RANK, 2 * PROBES + 9 * RANK), f32)

    def scalar_rows(rows):
        return ((rows, PROBES), f32)

    def tree(send, scalars_of, rows):
        got = exchange(send, planes)
        local = scalars_of()
        (z_send,) = call(
            functools.partial(plane_kernel, rows),
            [((DEPTH * (Z_ROWS + rows), PROBES), f32)],
            [got, local[-1]],
            2,
            1 << 20,
            name="plane",
        )
        z_got = exchange(z_send, depths)
        (back,) = call(
            functools.partial(depth_kernel, rows),
            [((PLANE * (ROWS + rows), PROBES), f32)],
            [got, z_got],
            2,
            1 << 20,
            name="depth",
        )
        return local, exchange(back, planes)

    (send,) = call(
        start_kernel,
        [message],
        [right_side, level_basis, coupling],
        60,
        1 << 26,
        scratch=[
            pltpu.VMEM(right_side.shape, f32),
            pltpu.VMEM((9, RANK, POINTS), bf16),
            pltpu.VMEM(coupling.shape, f32),
            message_scratch,
            pltpu.SemaphoreType.DMA((2 * HALVES + 2,)),
        ],
        name="start",
        far_ins=(0, 1, 2),
        far_outs=(0,),
    )
    (tile, image, parts, _), got = tree(
        send,
        lambda: call(
            tile_kernel,
            [((POINTS, POINTS), bf16), field, parts_block, scalar_rows(2)],
            [coordinates, tree_order, leaf_sizes, right_side, level_basis, coupling],
            12,
            4 << 30,
            scratch=[
                pltpu.VMEM((POINTS, POINTS), bf16),
                pltpu.VMEM((3, POINTS, 128), f32),
                pltpu.SemaphoreType.DMA((3,)),
            ],
            name="tile",
            far_outs=(0,),
        ),
        2,
    )
    residual, first_image, send, keep = call(
        turn_kernel,
        [field, field, message, scalar_rows(3)],
        [got, right_side, image, parts, level_basis, coupling],
        8,
        1 << 28,
        scratch=[message_scratch, pltpu.SemaphoreType.DMA((1,))],
        name="turn",
        far_outs=(2,),
    )
    (image, _), got = tree(
        send,
        lambda: call(
            leaf_kernel,
            [field, scalar_rows(3)],
            [leaf_sizes, residual, first_image, tile, level_basis, coupling],
            8,
            1 << 30,
            scratch=[
                pltpu.VMEM((POINTS, POINTS), bf16),
                pltpu.SemaphoreType.DMA((HALVES,)),
            ],
            name="leaf",
            far_ins=(3,),
        ),
        3,
    )
    return tuple(
        call(
            end_kernel,
            [field, field],
            [got, right_side, residual, first_image, image, level_basis, coupling, keep],
            8,
            1 << 28,
            scratch=[
                pltpu.VMEM(*field),
                pltpu.VMEM(*field),
                pltpu.SemaphoreType.DMA((HALVES + 1,)),
            ],
            name="end",
            far_outs=(0, 1),
        )
    )


def solution(mesh):
    in_specs = (
        P(None, "pts"),
        P(None, "pts"),
        P("pts", None),
        P("pts", None),
        P(None, None, "pts"),
        P("pts", None, None, None),
    )
    out_specs = (P(None, "pts"), P(None, "pts"))
    return jax.shard_map(
        on_device, mesh=mesh, in_specs=in_specs, out_specs=out_specs, check_vma=False
    )
```

```python
import functools

import jax
import jax.numpy as jnp
from jax import lax
from jax.experimental import pallas as pl
from jax.experimental.pallas import tpu as pltpu
from jax.sharding import PartitionSpec as P

f32 = jnp.float32
bf16 = jnp.bfloat16

SQRT_THREE = 1.7320508075688772
NOISE_VAR = 1.0

RANK = 32
PROBES = 128
POINTS = 1024
PLANE = 32
DEPTH = 16
ROWS = 18
Z_ROWS = 8
LEAST = 384
MOST = 640
HALVES = 2

NT = (((1,), (1,)), ((), ()))
TN = (((0,), (0,)), ((), ()))
NN = (((1,), (0,)), ((), ()))


def first_row(level):
    if level < 5:
        return 2 * (level - 1)
    return 16 if level == 5 else 8 + 2 * (level - 6)


def dot(a, b, dims):
    return lax.dot_general(a, b, dims, preferred_element_type=f32)


def halves(x):
    high = x.astype(bf16)
    return high, (x - high.astype(f32)).astype(bf16)


def dot_split(a, b, dims):
    a_high, a_low = halves(a)
    b_high, b_low = halves(b)
    a_dim, b_dim = dims[0][0][0], dims[0][1][0]
    return dot(
        jnp.concatenate([a_high, a_high, a_low], axis=a_dim),
        jnp.concatenate([b_high, b_low, b_high], axis=b_dim),
        dims,
    )


def project_split(wide, v):
    high, low = halves(v)
    return dot(wide, high, NT) + dot(wide, low, NT)


def rows_of(products):
    part = products[:, :PROBES]
    for start in range(PROBES, POINTS, PROBES):
        part = part + products[:, start : start + PROBES]
    return jnp.sum(part.T, axis=0, keepdims=True)


def down_rows(row):
    square = jnp.broadcast_to(row, (PROBES, PROBES)).T
    return jnp.concatenate([square] * (POINTS // PROBES), axis=1)


def row_ids(rows):
    return lax.broadcasted_iota(jnp.int32, (rows, PROBES), 0)


def send_levels(projected, coupling_ref, send_ref):
    for level in range(1, 10):
        own = coupling_ref[0, level, :RANK, :]
        partial = dot_split(own, projected[RANK * (level - 1) : RANK * level], TN)
        for half in range(2):
            send_ref[pl.ds(first_row(level) + half, PLANE, stride=ROWS), :] = partial[
                PLANE * half : PLANE * (half + 1)
            ]


def start_kernel(
    right_hbm, basis_hbm, coupling_hbm, send_hbm,
    right_ref, basis_ref, coupling_ref, send_ref, sems,
):
    width = POINTS // HALVES
    fetches = []
    for half in range(HALVES):
        span = pl.ds(width * half, width)
        right_copy = pltpu.make_async_copy(
            right_hbm.at[:, span], right_ref.at[:, span], sems.at[2 * half]
        )
        basis_copy = pltpu.make_async_copy(
            basis_hbm.at[pl.ds(1, 9), :, span],
            basis_ref.at[:, :, span],
            sems.at[2 * half + 1],
        )
        right_copy.start()
        basis_copy.start()
        fetches.append((right_copy, basis_copy))
    factors = pltpu.make_async_copy(coupling_hbm, coupling_ref, sems.at[2 * HALVES])
    factors.start()
    projected = None
    for half, (right_copy, basis_copy) in enumerate(fetches):
        span = slice(width * half, width * (half + 1))
        right_copy.wait()
        basis_copy.wait()
        part = dot(
            basis_ref[:, :, span].reshape(9 * RANK, width),
            right_ref[:, span].astype(bf16),
            NT,
        )
        projected = part if half == 0 else projected + part
    factors.wait()
    send_levels(projected, coupling_ref, send_ref)
    out = pltpu.make_async_copy(send_ref, send_hbm, sems.at[2 * HALVES + 1])
    out.start()
    out.wait()


def leaf_level(v, rounded, leaf, boundary, basis_ref, coupling_ref):
    wide = basis_ref[0].astype(f32)
    in_first = lax.broadcasted_iota(jnp.int32, (RANK, POINTS), 1) < boundary
    both = jnp.concatenate(
        [jnp.where(in_first, wide, 0.0), jnp.where(in_first, 0.0, wide)], axis=0
    ).astype(bf16)
    factor = coupling_ref[0, 0]
    mixed = dot_split(factor, dot(both, rounded, NT), TN)
    coefficients = dot_split(factor, mixed, NN).astype(bf16)
    image = leaf + dot(coefficients, both, TN)
    curvature = rows_of(v * leaf) + jnp.sum(mixed * mixed, axis=0, keepdims=True)
    return image, curvature


def tile_kernel(
    coordinates_ref, order_ref, sizes_ref, right_ref, basis_ref, coupling_ref,
    tile_hbm, image_ref, parts_ref, scalars_ref,
    tile_ref, sems,
):
    boundary = sizes_ref[0, 0]
    order = order_ref[...]
    place, segment = jnp.bitwise_and(order, 127), jnp.right_shift(order, 7)
    sources = [
        jnp.concatenate(
            [coordinates_ref[:, start : start + 128], jnp.zeros((5, 128), f32)], axis=0
        )
        for start in range(0, POINTS, 128)
    ]
    pieces = []
    for start in range(0, POINTS, 128):
        lane = jnp.broadcast_to(place[:, start : start + 128], (8, 128))
        chosen = jnp.broadcast_to(segment[:, start : start + 128], (8, 128))
        piece = jnp.zeros((8, 128), f32)
        for number, source in enumerate(sources):
            piece = jnp.where(chosen == number, jnp.take_along_axis(source, lane, axis=1), piece)
        pieces.append(piece)
    x = jnp.concatenate(pieces, axis=1)
    x = SQRT_THREE * x
    column = x.T
    edge = boundary.astype(f32) - 0.5
    block = 128
    last = POINTS // block
    tile_ref[:LEAST, MOST:] = jnp.zeros((LEAST, POINTS - MOST), bf16)
    tile_ref[MOST:, :LEAST] = jnp.zeros((POINTS - MOST, LEAST), bf16)
    ids = lax.broadcasted_iota(jnp.int32, (block, block), 0)
    lanes = lax.broadcasted_iota(jnp.int32, (block, block), 1)
    diagonal = jnp.where(ids == lanes, NOISE_VAR, 0.0)
    row_side = ids.astype(f32) - edge
    col_side = lanes.astype(f32) - edge
    least, most = LEAST // block, MOST // block
    copies = []
    for up in range(last):
        rows = slice(block * up, block * (up + 1))
        down = [
            jnp.broadcast_to(column[rows, c : c + 1], (block, block)) for c in range(3)
        ]
        for across in range(up, most if up < least else last):
            columns = slice(block * across, block * (across + 1))
            dist_sq = None
            for c in range(3):
                offset = down[c] - x[c : c + 1, columns]
                dist_sq = offset * offset if c == 0 else dist_sq + offset * offset
            scaled = dist_sq * lax.rsqrt(jnp.maximum(dist_sq, 1e-37))
            values = (1.0 + scaled) * jnp.exp(-scaled)
            if across >= least and up < most:
                same = (row_side + block * up) * (col_side + block * across) > 0.0
                values = jnp.where(same, values, 0.0)
            if across == up:
                values = values + diagonal
            tile_ref[rows, columns] = values.astype(bf16)
            if across != up:
                tile_ref[columns, rows] = values.T.astype(bf16)
        span = pl.ds(block * up, block)
        copies.append(
            pltpu.make_async_copy(tile_ref.at[span], tile_hbm.at[span], sems.at[up])
        )
        copies[-1].start()

    v = right_ref[...]
    rounded = v.astype(bf16)
    leaf = dot(rounded, tile_ref[...], NN)
    image, curvature = leaf_level(v, rounded, leaf, boundary, basis_ref, coupling_ref)
    image_ref[...] = image
    scalars_ref[0:1, :] = curvature
    scalars_ref[1:2, :] = rows_of(v * v)
    wide = basis_ref[1:10].reshape(9 * RANK, POINTS)
    parts_ref[:, :PROBES] = project_split(wide, v)
    parts_ref[:, PROBES : 2 * PROBES] = project_split(wide, image)
    parts_ref[:, 2 * PROBES :] = dot(wide, wide, NT)
    for copy in copies:
        copy.wait()


def leaf_kernel(
    sizes_ref, residual_ref, first_image_ref, tile_hbm, basis_ref, coupling_ref,
    image_ref, scalars_ref, tile_ref, sems,
):
    width = POINTS // HALVES
    copies = []
    for half in range(HALVES):
        rows = pl.ds(width * half, width)
        copies.append(pltpu.make_async_copy(tile_hbm.at[rows], tile_ref.at[rows], sems.at[half]))
        copies[-1].start()
    v = residual_ref[...]
    rounded = v.astype(bf16)
    leaf = None
    for half in range(HALVES):
        span = slice(width * half, width * (half + 1))
        copies[half].wait()
        part = dot(rounded[:, span], tile_ref[span, :], NN)
        leaf = part if half == 0 else leaf + part
    image, curvature = leaf_level(
        v, rounded, leaf, sizes_ref[0, 0], basis_ref, coupling_ref
    )
    image_ref[...] = image
    scalars_ref[0:1, :] = curvature
    scalars_ref[1:2, :] = rows_of(v * v)
    scalars_ref[2:3, :] = rows_of(v * first_image_ref[...])


def pair_sums(got_ref):
    sums = [[got_ref[ROWS * d : ROWS * d + 8, :] for d in range(PLANE)]]
    for _ in range(4):
        last = sums[-1]
        sums.append([last[2 * i] + last[2 * i + 1] for i in range(len(last) // 2)])
    return sums


def total(got_ref, count, stride, start, rows):
    parts = [got_ref[stride * d + start : stride * d + start + rows, :] for d in range(count)]
    while len(parts) > 1:
        parts = [parts[2 * i] + parts[2 * i + 1] for i in range(len(parts) // 2)]
    return parts[0]


def squares(nodes):
    result = nodes[0] * nodes[0]
    for node in nodes[1:]:
        result = result + node * node
    return result


def plane_kernel(count, got_ref, scalars_ref, send_ref):
    ids = row_ids(8)
    sums = pair_sums(got_ref)
    square = jnp.zeros((8, PROBES), f32)
    for level in range(1, 5):
        square = jnp.where(ids // 2 == level - 1, squares(sums[level]), square)
    fifth = total(got_ref, PLANE, ROWS, 16, 2)
    curvature = jnp.sum(square, axis=0, keepdims=True) + jnp.sum(
        fifth * fifth, axis=0, keepdims=True
    )
    scalars = scalars_ref[...] + jnp.where(row_ids(count) == 0, curvature, 0.0)
    block = jnp.concatenate([total(got_ref, PLANE, ROWS, 8, 8), scalars], axis=0)
    stride = Z_ROWS + count
    for z in range(DEPTH):
        send_ref[stride * z : stride * (z + 1), :] = block


def depth_kernel(count, got_ref, z_got_ref, send_ref):
    z_stride, stride = Z_ROWS + count, ROWS + count
    own = lax.axis_index("pts") // PLANE
    ids = row_ids(8)
    reach = jnp.left_shift(2, ids // 2)
    pair = jnp.zeros((8, PROBES), f32)
    nodes = []
    for z in range(DEPTH):
        block = z_got_ref[z_stride * z : z_stride * z + 8, :]
        nodes.append(block)
        apart = jnp.bitwise_xor(own, z)
        pair = pair + jnp.where(apart < reach, block, 0.0)
    square = jnp.zeros((8, PROBES), f32)
    for level in range(4):
        nodes = [nodes[2 * i] + nodes[2 * i + 1] for i in range(len(nodes) // 2)]
        square = jnp.where(ids // 2 == level, squares(nodes), square)
    curvature = jnp.sum(square, axis=0, keepdims=True)
    scalars = total(z_got_ref, DEPTH, z_stride, 8, count)
    scalars = scalars + jnp.where(row_ids(count) == 0, curvature, 0.0)
    tail = jnp.concatenate([pair, total(got_ref, PLANE, ROWS, 16, 2), scalars], axis=0)
    sums = pair_sums(got_ref)
    for d in range(PLANE):
        first = sums[4][d >> 4]
        for level in (3, 2, 1):
            first = jnp.where(ids // 2 == level - 1, sums[level][d >> level], first)
        send_ref[stride * d : stride * d + 8, :] = first
        send_ref[stride * d + 8 : stride * (d + 1), :] = tail


def level_coefficients(got_ref, coupling_ref, stride):
    coefficients = []
    for level in range(1, 10):
        mixed = jnp.concatenate(
            [
                got_ref[pl.ds(first_row(level) + half, PLANE, stride=stride), :]
                for half in range(2)
            ],
            axis=0,
        )
        coefficients.append(dot_split(coupling_ref[0, level, :RANK, :], mixed, NN))
    return jnp.concatenate(coefficients, axis=0).astype(bf16)


def expand(coefficients, basis_ref, span):
    width = span.stop - span.start
    return dot(coefficients, basis_ref[1:10, :, span].reshape(9 * RANK, width), TN)


def turn_kernel(
    got_ref, right_ref, image_ref, parts_ref, basis_ref, coupling_ref,
    residual_ref, whole_image_ref, send_hbm, keep_ref, send_ref, sem,
):
    scalars = total(got_ref, PLANE, ROWS + 2, ROWS, 2)
    curvature, norm = scalars[0:1], scalars[1:2]
    step = norm / curvature
    coefficients = level_coefficients(got_ref, coupling_ref, ROWS + 2)
    gram_high, gram_low = halves(parts_ref[:, 2 * PROBES :])
    spread = dot(gram_high, coefficients, NN) + dot(gram_low, coefficients, NN)
    projected = parts_ref[:, :PROBES] - step * (parts_ref[:, PROBES : 2 * PROBES] + spread)
    send_levels(projected, coupling_ref, send_ref)
    out = pltpu.make_async_copy(send_ref, send_hbm, sem.at[0])
    out.start()
    whole = image_ref[...] + expand(coefficients, basis_ref, slice(0, POINTS))
    whole_image_ref[...] = whole
    residual_ref[...] = right_ref[...] - down_rows(step) * whole
    keep_ref[0:1, :] = step
    keep_ref[1:2, :] = curvature
    keep_ref[2:3, :] = norm
    out.wait()


def end_kernel(
    got_ref, right_ref, residual_ref, first_image_ref, image_ref, basis_ref, coupling_ref,
    keep_ref, solution_hbm, last_hbm, solution_ref, last_ref, sems,
):
    scalars = total(got_ref, PLANE, ROWS + 3, ROWS, 3)
    own, norm, cross = scalars[0:1], scalars[1:2], scalars[2:3]
    step, curvature, norm_before = keep_ref[0:1, :], keep_ref[1:2, :], keep_ref[2:3, :]
    ratio = norm / norm_before
    step_now = norm / (own + 2.0 * ratio * cross + ratio * ratio * curvature)
    ratio_down, step_down = down_rows(ratio), down_rows(step_now)
    right, residual = right_ref[...], residual_ref[...]
    direction = residual + ratio_down * right
    solution_ref[...] = down_rows(step) * right + step_down * direction
    copies = [pltpu.make_async_copy(solution_ref, solution_hbm, sems.at[HALVES])]
    copies[0].start()
    coefficients = level_coefficients(got_ref, coupling_ref, ROWS + 3)
    width = POINTS // HALVES
    for half in range(HALVES):
        span = slice(width * half, width * (half + 1))
        image = image_ref[:, span] + expand(coefficients, basis_ref, span)
        image = image + ratio_down[:, span] * first_image_ref[:, span]
        last_ref[:, span] = residual[:, span] - step_down[:, span] * image
        columns = pl.ds(width * half, width)
        copies.append(
            pltpu.make_async_copy(
                last_ref.at[:, columns], last_hbm.at[:, columns], sems.at[half]
            )
        )
        copies[-1].start()
    for copy in copies:
        copy.wait()


VMEM = pl.BlockSpec(memory_space=pltpu.VMEM)
SMEM = pl.BlockSpec(memory_space=pltpu.SMEM)
HBM = pl.BlockSpec(memory_space=pltpu.HBM)


def call(body, outs, ins, megabytes, cost, scratch=(), name=None, far_ins=(), far_outs=()):
    specs = [SMEM if a.dtype == jnp.int32 and a.shape == (1, 2) else VMEM for a in ins]
    for place in far_ins:
        specs[place] = HBM
    return pl.pallas_call(
        body,
        out_shape=[
            (pltpu.HBM if place in far_outs else jax.ShapeDtypeStruct)(shape, kind)
            for place, (shape, kind) in enumerate(outs)
        ],
        in_specs=specs,
        out_specs=[HBM if place in far_outs else VMEM for place in range(len(outs))],
        scratch_shapes=list(scratch),
        compiler_params=pltpu.CompilerParams(vmem_limit_bytes=megabytes << 20),
        cost_estimate=pl.CostEstimate(flops=cost, bytes_accessed=2 << 20, transcendentals=0),
        name=name,
    )(*ins)


def plane_groups(count):
    return [list(range(PLANE * z, PLANE * (z + 1))) for z in range(count // PLANE)]


def depth_groups(count):
    return [list(range(place, count, PLANE)) for place in range(PLANE)]


def exchange(rows, groups):
    members = len(groups[0])
    blocks = rows.reshape(members, 1, rows.shape[0] // members * PROBES)
    got = lax.all_to_all(blocks, "pts", 0, 0, axis_index_groups=groups)
    return got.reshape(rows.shape)


def on_device(right_side, coordinates, tree_order, leaf_sizes, level_basis, coupling):
    count = lax.axis_size("pts")
    planes, depths = plane_groups(count), depth_groups(count)
    field = ((PROBES, POINTS), f32)
    message = ((PLANE * ROWS, PROBES), f32)
    message_scratch = pltpu.VMEM(*message)
    parts_block = ((9 * RANK, 2 * PROBES + 9 * RANK), f32)

    def scalar_rows(rows):
        return ((rows, PROBES), f32)

    def tree(send, scalars_of, rows):
        got = exchange(send, planes)
        local = scalars_of()
        (z_send,) = call(
            functools.partial(plane_kernel, rows),
            [((DEPTH * (Z_ROWS + rows), PROBES), f32)],
            [got, local[-1]],
            2,
            1 << 20,
            name="plane",
        )
        z_got = exchange(z_send, depths)
        (back,) = call(
            functools.partial(depth_kernel, rows),
            [((PLANE * (ROWS + rows), PROBES), f32)],
            [got, z_got],
            2,
            1 << 20,
            name="depth",
        )
        return local, exchange(back, planes)

    (send,) = call(
        start_kernel,
        [message],
        [right_side, level_basis, coupling],
        60,
        1 << 26,
        scratch=[
            pltpu.VMEM(right_side.shape, f32),
            pltpu.VMEM((9, RANK, POINTS), bf16),
            pltpu.VMEM(coupling.shape, f32),
            message_scratch,
            pltpu.SemaphoreType.DMA((2 * HALVES + 2,)),
        ],
        name="start",
        far_ins=(0, 1, 2),
        far_outs=(0,),
    )
    (tile, image, parts, _), got = tree(
        send,
        lambda: call(
            tile_kernel,
            [((POINTS, POINTS), bf16), field, parts_block, scalar_rows(2)],
            [coordinates, tree_order, leaf_sizes, right_side, level_basis, coupling],
            12,
            4 << 30,
            scratch=[
                pltpu.VMEM((POINTS, POINTS), bf16),
                pltpu.SemaphoreType.DMA((POINTS // 128,)),
            ],
            name="tile",
            far_outs=(0,),
        ),
        2,
    )
    residual, first_image, send, keep = call(
        turn_kernel,
        [field, field, message, scalar_rows(3)],
        [got, right_side, image, parts, level_basis, coupling],
        8,
        1 << 28,
        scratch=[message_scratch, pltpu.SemaphoreType.DMA((1,))],
        name="turn",
        far_outs=(2,),
    )
    (image, _), got = tree(
        send,
        lambda: call(
            leaf_kernel,
            [field, scalar_rows(3)],
            [leaf_sizes, residual, first_image, tile, level_basis, coupling],
            8,
            1 << 30,
            scratch=[
                pltpu.VMEM((POINTS, POINTS), bf16),
                pltpu.SemaphoreType.DMA((HALVES,)),
            ],
            name="leaf",
            far_ins=(3,),
        ),
        3,
    )
    return tuple(
        call(
            end_kernel,
            [field, field],
            [got, right_side, residual, first_image, image, level_basis, coupling, keep],
            8,
            1 << 28,
            scratch=[
                pltpu.VMEM(*field),
                pltpu.VMEM(*field),
                pltpu.SemaphoreType.DMA((HALVES + 1,)),
            ],
            name="end",
            far_outs=(0, 1),
        )
    )


def solution(mesh):
    in_specs = (
        P(None, "pts"),
        P(None, "pts"),
        P("pts", None),
        P("pts", None),
        P(None, None, "pts"),
        P("pts", None, None, None),
    )
    out_specs = (P(None, "pts"), P(None, "pts"))
    return jax.shard_map(
        on_device, mesh=mesh, in_specs=in_specs, out_specs=out_specs, check_vma=False
    )
```

```python
import functools

import jax
import jax.numpy as jnp
from jax import lax
from jax.experimental import pallas as pl
from jax.experimental.pallas import tpu as pltpu
from jax.sharding import PartitionSpec as P

f32 = jnp.float32
bf16 = jnp.bfloat16

SQRT_THREE = 1.7320508075688772
NOISE_VAR = 1.0

RANK = 32
PROBES = 128
POINTS = 1024
PLANE = 32
DEPTH = 16
ROWS = 18
Z_ROWS = 8
LEAST = 384
MOST = 640
HALVES = 2
PARTS = 2 * PROBES + 9 * RANK

NT = (((1,), (1,)), ((), ()))
TN = (((0,), (0,)), ((), ()))
NN = (((1,), (0,)), ((), ()))


def first_row(level):
    if level < 5:
        return 2 * (level - 1)
    return 16 if level == 5 else 8 + 2 * (level - 6)


def dot(a, b, dims):
    return lax.dot_general(a, b, dims, preferred_element_type=f32)


def halves(x):
    high = x.astype(bf16)
    return high, (x - high.astype(f32)).astype(bf16)


def dot_split(a, b, dims):
    a_high, a_low = halves(a)
    b_high, b_low = halves(b)
    a_dim, b_dim = dims[0][0][0], dims[0][1][0]
    return dot(
        jnp.concatenate([a_high, a_high, a_low], axis=a_dim),
        jnp.concatenate([b_high, b_low, b_high], axis=b_dim),
        dims,
    )


def project_split(wide, v):
    high, low = halves(v)
    return dot(wide, high, NT) + dot(wide, low, NT)


def rows_of(products):
    part = products[:, :PROBES]
    for start in range(PROBES, POINTS, PROBES):
        part = part + products[:, start : start + PROBES]
    return jnp.sum(part.T, axis=0, keepdims=True)


def down_rows(row):
    square = jnp.broadcast_to(row, (PROBES, PROBES)).T
    return jnp.concatenate([square] * (POINTS // PROBES), axis=1)


def row_ids(rows):
    return lax.broadcasted_iota(jnp.int32, (rows, PROBES), 0)


def send_levels(projected, coupling_ref, send_ref):
    for level in range(1, 10):
        own = coupling_ref[0, level, :RANK, :]
        partial = dot_split(own, projected[RANK * (level - 1) : RANK * level], TN)
        for half in range(2):
            send_ref[pl.ds(first_row(level) + half, PLANE, stride=ROWS), :] = partial[
                PLANE * half : PLANE * (half + 1)
            ]


def start_kernel(
    right_hbm, basis_hbm, coupling_hbm, send_hbm,
    right_ref, basis_ref, coupling_ref, send_ref, sems,
):
    width = POINTS // HALVES
    fetches = []
    for half in range(HALVES):
        span = pl.ds(width * half, width)
        right_copy = pltpu.make_async_copy(
            right_hbm.at[:, span], right_ref.at[:, span], sems.at[2 * half]
        )
        basis_copy = pltpu.make_async_copy(
            basis_hbm.at[pl.ds(1, 9), :, span],
            basis_ref.at[:, :, span],
            sems.at[2 * half + 1],
        )
        right_copy.start()
        basis_copy.start()
        fetches.append((right_copy, basis_copy))
    factors = pltpu.make_async_copy(coupling_hbm, coupling_ref, sems.at[2 * HALVES])
    factors.start()
    projected = None
    for half, (right_copy, basis_copy) in enumerate(fetches):
        span = slice(width * half, width * (half + 1))
        right_copy.wait()
        basis_copy.wait()
        part = dot(
            basis_ref[:, :, span].reshape(9 * RANK, width),
            right_ref[:, span].astype(bf16),
            NT,
        )
        projected = part if half == 0 else projected + part
    factors.wait()
    send_levels(projected, coupling_ref, send_ref)
    out = pltpu.make_async_copy(send_ref, send_hbm, sems.at[2 * HALVES + 1])
    out.start()
    out.wait()


def leaf_product(rounded, tile_ref):
    return jnp.concatenate(
        [
            dot(rounded[:, :MOST], tile_ref[:MOST, :LEAST], NN),
            dot(rounded, tile_ref[:, LEAST:MOST], NN),
            dot(rounded[:, LEAST:], tile_ref[LEAST:, MOST:], NN),
        ],
        axis=1,
    )


def leaf_level(v, rounded, leaf, boundary, basis_ref, coupling_ref):
    wide = basis_ref[0].astype(f32)
    in_first = lax.broadcasted_iota(jnp.int32, (RANK, POINTS), 1) < boundary
    both = jnp.concatenate(
        [jnp.where(in_first, wide, 0.0), jnp.where(in_first, 0.0, wide)], axis=0
    ).astype(bf16)
    factor = coupling_ref[0, 0]
    mixed = dot_split(factor, dot(both, rounded, NT), TN)
    coefficients = dot_split(factor, mixed, NN).astype(bf16)
    image = leaf + dot(coefficients, both, TN)
    curvature = rows_of(v * leaf) + jnp.sum(mixed * mixed, axis=0, keepdims=True)
    return image, curvature


def tile_kernel(
    coordinates_ref, order_ref, sizes_ref, right_ref, basis_ref, coupling_ref,
    tile_hbm, image_ref, parts_hbm, scalars_ref,
    tile_ref, parts_ref, sems,
):
    boundary = sizes_ref[0, 0]
    order = order_ref[...]
    place, segment = jnp.bitwise_and(order, 127), jnp.right_shift(order, 7)
    sources = [
        jnp.concatenate(
            [coordinates_ref[:, start : start + 128], jnp.zeros((5, 128), f32)], axis=0
        )
        for start in range(0, POINTS, 128)
    ]
    pieces = []
    for start in range(0, POINTS, 128):
        lane = jnp.broadcast_to(place[:, start : start + 128], (8, 128))
        chosen = jnp.broadcast_to(segment[:, start : start + 128], (8, 128))
        piece = jnp.zeros((8, 128), f32)
        for number, source in enumerate(sources):
            piece = jnp.where(chosen == number, jnp.take_along_axis(source, lane, axis=1), piece)
        pieces.append(piece)
    x = jnp.concatenate(pieces, axis=1)
    x = SQRT_THREE * x
    column = x.T
    edge = boundary.astype(f32) - 0.5
    block = 128
    last = POINTS // block
    tile_ref[:LEAST, MOST:] = jnp.zeros((LEAST, POINTS - MOST), bf16)
    tile_ref[MOST:, :LEAST] = jnp.zeros((POINTS - MOST, LEAST), bf16)
    ids = lax.broadcasted_iota(jnp.int32, (block, block), 0)
    lanes = lax.broadcasted_iota(jnp.int32, (block, block), 1)
    diagonal = jnp.where(ids == lanes, NOISE_VAR, 0.0)
    row_side = ids.astype(f32) - edge
    col_side = lanes.astype(f32) - edge
    least, most = LEAST // block, MOST // block
    copies = []
    for up in range(last):
        rows = slice(block * up, block * (up + 1))
        down = [
            jnp.broadcast_to(column[rows, c : c + 1], (block, block)) for c in range(3)
        ]
        for across in range(up, most if up < least else last):
            columns = slice(block * across, block * (across + 1))
            dist_sq = None
            for c in range(3):
                offset = down[c] - x[c : c + 1, columns]
                dist_sq = offset * offset if c == 0 else dist_sq + offset * offset
            scaled = dist_sq * lax.rsqrt(jnp.maximum(dist_sq, 1e-37))
            values = (1.0 + scaled) * jnp.exp(-scaled)
            if across >= least and up < most:
                same = (row_side + block * up) * (col_side + block * across) > 0.0
                values = jnp.where(same, values, 0.0)
            if across == up:
                values = values + diagonal
            tile_ref[rows, columns] = values.astype(bf16)
            if across != up:
                tile_ref[columns, rows] = values.T.astype(bf16)
        span = pl.ds(block * up, block)
        copies.append(
            pltpu.make_async_copy(tile_ref.at[span], tile_hbm.at[span], sems.at[up])
        )
        copies[-1].start()

    def send_parts(start, stop):
        lanes = pl.ds(start, stop - start)
        copies.append(
            pltpu.make_async_copy(
                parts_ref.at[:, lanes], parts_hbm.at[:, lanes], sems.at[len(copies)]
            )
        )
        copies[-1].start()

    v = right_ref[...]
    wide = basis_ref[1:10].reshape(9 * RANK, POINTS)
    parts_ref[:, PROBES : 2 * PROBES] = project_split(wide, v)
    parts_ref[:, 2 * PROBES :] = dot(wide, wide, NT)
    send_parts(PROBES, PARTS)
    rounded = v.astype(bf16)
    leaf = leaf_product(rounded, tile_ref)
    image, curvature = leaf_level(v, rounded, leaf, boundary, basis_ref, coupling_ref)
    parts_ref[:, :PROBES] = project_split(wide, image)
    send_parts(0, PROBES)
    image_ref[...] = image
    scalars_ref[0:1, :] = curvature
    scalars_ref[1:2, :] = rows_of(v * v)
    for copy in copies:
        copy.wait()


def leaf_kernel(
    sizes_ref, residual_ref, first_image_ref, tile_hbm, basis_ref, coupling_ref,
    image_ref, scalars_ref, tile_ref, sems,
):
    width = POINTS // HALVES
    copies = []
    for half in range(HALVES):
        rows = pl.ds(width * half, width)
        copies.append(pltpu.make_async_copy(tile_hbm.at[rows], tile_ref.at[rows], sems.at[half]))
        copies[-1].start()
    v = residual_ref[...]
    rounded = v.astype(bf16)
    for copy in copies:
        copy.wait()
    leaf = leaf_product(rounded, tile_ref)
    image, curvature = leaf_level(
        v, rounded, leaf, sizes_ref[0, 0], basis_ref, coupling_ref
    )
    image_ref[...] = image
    scalars_ref[0:1, :] = curvature
    scalars_ref[1:2, :] = rows_of(v * v)
    scalars_ref[2:3, :] = rows_of(v * first_image_ref[...])


def pair_sums(got_ref):
    sums = [[got_ref[ROWS * d : ROWS * d + 8, :] for d in range(PLANE)]]
    for _ in range(4):
        last = sums[-1]
        sums.append([last[2 * i] + last[2 * i + 1] for i in range(len(last) // 2)])
    return sums


def total(got_ref, count, stride, start, rows):
    parts = [got_ref[stride * d + start : stride * d + start + rows, :] for d in range(count)]
    while len(parts) > 1:
        parts = [parts[2 * i] + parts[2 * i + 1] for i in range(len(parts) // 2)]
    return parts[0]


def squares(nodes):
    result = nodes[0] * nodes[0]
    for node in nodes[1:]:
        result = result + node * node
    return result


def plane_kernel(count, got_ref, scalars_ref, send_ref):
    ids = row_ids(8)
    sums = pair_sums(got_ref)
    square = jnp.zeros((8, PROBES), f32)
    for level in range(1, 5):
        square = jnp.where(ids // 2 == level - 1, squares(sums[level]), square)
    fifth = total(got_ref, PLANE, ROWS, 16, 2)
    curvature = jnp.sum(square, axis=0, keepdims=True) + jnp.sum(
        fifth * fifth, axis=0, keepdims=True
    )
    scalars = scalars_ref[...] + jnp.where(row_ids(count) == 0, curvature, 0.0)
    block = jnp.concatenate([total(got_ref, PLANE, ROWS, 8, 8), scalars], axis=0)
    stride = Z_ROWS + count
    for z in range(DEPTH):
        send_ref[stride * z : stride * (z + 1), :] = block


def depth_kernel(count, got_ref, z_got_ref, send_ref):
    z_stride, stride = Z_ROWS + count, ROWS + count
    own = lax.axis_index("pts") // PLANE
    ids = row_ids(8)
    reach = jnp.left_shift(2, ids // 2)
    pair = jnp.zeros((8, PROBES), f32)
    nodes = []
    for z in range(DEPTH):
        block = z_got_ref[z_stride * z : z_stride * z + 8, :]
        nodes.append(block)
        apart = jnp.bitwise_xor(own, z)
        pair = pair + jnp.where(apart < reach, block, 0.0)
    square = jnp.zeros((8, PROBES), f32)
    for level in range(4):
        nodes = [nodes[2 * i] + nodes[2 * i + 1] for i in range(len(nodes) // 2)]
        square = jnp.where(ids // 2 == level, squares(nodes), square)
    curvature = jnp.sum(square, axis=0, keepdims=True)
    scalars = total(z_got_ref, DEPTH, z_stride, 8, count)
    scalars = scalars + jnp.where(row_ids(count) == 0, curvature, 0.0)
    tail = jnp.concatenate([pair, total(got_ref, PLANE, ROWS, 16, 2), scalars], axis=0)
    sums = pair_sums(got_ref)
    for d in range(PLANE):
        first = sums[4][d >> 4]
        for level in (3, 2, 1):
            first = jnp.where(ids // 2 == level - 1, sums[level][d >> level], first)
        send_ref[stride * d : stride * d + 8, :] = first
        send_ref[stride * d + 8 : stride * (d + 1), :] = tail


def level_coefficients(got_ref, coupling_ref, stride):
    coefficients = []
    for level in range(1, 10):
        mixed = jnp.concatenate(
            [
                got_ref[pl.ds(first_row(level) + half, PLANE, stride=stride), :]
                for half in range(2)
            ],
            axis=0,
        )
        coefficients.append(dot_split(coupling_ref[0, level, :RANK, :], mixed, NN))
    return jnp.concatenate(coefficients, axis=0).astype(bf16)


def expand(coefficients, basis_ref, span):
    width = span.stop - span.start
    return dot(coefficients, basis_ref[1:10, :, span].reshape(9 * RANK, width), TN)


def turn_kernel(
    got_ref, right_ref, image_ref, parts_ref, basis_ref, coupling_ref,
    residual_ref, whole_image_ref, send_hbm, keep_ref, send_ref, sem,
):
    scalars = total(got_ref, PLANE, ROWS + 2, ROWS, 2)
    curvature, norm = scalars[0:1], scalars[1:2]
    step = norm / curvature
    coefficients = level_coefficients(got_ref, coupling_ref, ROWS + 2)
    gram_high, gram_low = halves(parts_ref[:, 2 * PROBES :])
    spread = dot(gram_high, coefficients, NN) + dot(gram_low, coefficients, NN)
    projected = parts_ref[:, PROBES : 2 * PROBES] - step * (parts_ref[:, :PROBES] + spread)
    send_levels(projected, coupling_ref, send_ref)
    out = pltpu.make_async_copy(send_ref, send_hbm, sem.at[0])
    out.start()
    whole = image_ref[...] + expand(coefficients, basis_ref, slice(0, POINTS))
    whole_image_ref[...] = whole
    residual_ref[...] = right_ref[...] - down_rows(step) * whole
    keep_ref[0:1, :] = step
    keep_ref[1:2, :] = curvature
    keep_ref[2:3, :] = norm
    out.wait()


def end_kernel(
    got_ref, right_ref, residual_ref, first_image_ref, image_ref, basis_ref, coupling_ref,
    keep_ref, solution_hbm, last_hbm, solution_ref, last_ref, sems,
):
    scalars = total(got_ref, PLANE, ROWS + 3, ROWS, 3)
    own, norm, cross = scalars[0:1], scalars[1:2], scalars[2:3]
    step, curvature, norm_before = keep_ref[0:1, :], keep_ref[1:2, :], keep_ref[2:3, :]
    ratio = norm / norm_before
    step_now = norm / (own + 2.0 * ratio * cross + ratio * ratio * curvature)
    ratio_down, step_down = down_rows(ratio), down_rows(step_now)
    right, residual = right_ref[...], residual_ref[...]
    direction = residual + ratio_down * right
    solution_ref[...] = down_rows(step) * right + step_down * direction
    copies = [pltpu.make_async_copy(solution_ref, solution_hbm, sems.at[HALVES])]
    copies[0].start()
    coefficients = level_coefficients(got_ref, coupling_ref, ROWS + 3)
    width = POINTS // HALVES
    for half in range(HALVES):
        span = slice(width * half, width * (half + 1))
        image = image_ref[:, span] + expand(coefficients, basis_ref, span)
        image = image + ratio_down[:, span] * first_image_ref[:, span]
        last_ref[:, span] = residual[:, span] - step_down[:, span] * image
        columns = pl.ds(width * half, width)
        copies.append(
            pltpu.make_async_copy(
                last_ref.at[:, columns], last_hbm.at[:, columns], sems.at[half]
            )
        )
        copies[-1].start()
    for copy in copies:
        copy.wait()


VMEM = pl.BlockSpec(memory_space=pltpu.VMEM)
SMEM = pl.BlockSpec(memory_space=pltpu.SMEM)
HBM = pl.BlockSpec(memory_space=pltpu.HBM)


def call(body, outs, ins, megabytes, cost, scratch=(), name=None, far_ins=(), far_outs=()):
    specs = [SMEM if a.dtype == jnp.int32 and a.shape == (1, 2) else VMEM for a in ins]
    for place in far_ins:
        specs[place] = HBM
    return pl.pallas_call(
        body,
        out_shape=[
            (pltpu.HBM if place in far_outs else jax.ShapeDtypeStruct)(shape, kind)
            for place, (shape, kind) in enumerate(outs)
        ],
        in_specs=specs,
        out_specs=[HBM if place in far_outs else VMEM for place in range(len(outs))],
        scratch_shapes=list(scratch),
        compiler_params=pltpu.CompilerParams(vmem_limit_bytes=megabytes << 20),
        cost_estimate=pl.CostEstimate(flops=cost, bytes_accessed=2 << 20, transcendentals=0),
        name=name,
    )(*ins)


def plane_groups(count):
    return [list(range(PLANE * z, PLANE * (z + 1))) for z in range(count // PLANE)]


def depth_groups(count):
    return [list(range(place, count, PLANE)) for place in range(PLANE)]


def exchange(rows, groups):
    members = len(groups[0])
    blocks = rows.reshape(members, 1, rows.shape[0] // members * PROBES)
    got = lax.all_to_all(blocks, "pts", 0, 0, axis_index_groups=groups)
    return got.reshape(rows.shape)


def on_device(right_side, coordinates, tree_order, leaf_sizes, level_basis, coupling):
    count = lax.axis_size("pts")
    planes, depths = plane_groups(count), depth_groups(count)
    field = ((PROBES, POINTS), f32)
    message = ((PLANE * ROWS, PROBES), f32)
    message_scratch = pltpu.VMEM(*message)
    parts_block = ((9 * RANK, PARTS), f32)

    def scalar_rows(rows):
        return ((rows, PROBES), f32)

    def tree(send, scalars_of, rows):
        got = exchange(send, planes)
        local = scalars_of()
        (z_send,) = call(
            functools.partial(plane_kernel, rows),
            [((DEPTH * (Z_ROWS + rows), PROBES), f32)],
            [got, local[-1]],
            2,
            1 << 20,
            name="plane",
        )
        z_got = exchange(z_send, depths)
        (back,) = call(
            functools.partial(depth_kernel, rows),
            [((PLANE * (ROWS + rows), PROBES), f32)],
            [got, z_got],
            2,
            1 << 20,
            name="depth",
        )
        return local, exchange(back, planes)

    (send,) = call(
        start_kernel,
        [message],
        [right_side, level_basis, coupling],
        60,
        1 << 26,
        scratch=[
            pltpu.VMEM(right_side.shape, f32),
            pltpu.VMEM((9, RANK, POINTS), bf16),
            pltpu.VMEM(coupling.shape, f32),
            message_scratch,
            pltpu.SemaphoreType.DMA((2 * HALVES + 2,)),
        ],
        name="start",
        far_ins=(0, 1, 2),
        far_outs=(0,),
    )
    (tile, image, parts, _), got = tree(
        send,
        lambda: call(
            tile_kernel,
            [((POINTS, POINTS), bf16), field, parts_block, scalar_rows(2)],
            [coordinates, tree_order, leaf_sizes, right_side, level_basis, coupling],
            12,
            4 << 30,
            scratch=[
                pltpu.VMEM((POINTS, POINTS), bf16),
                pltpu.VMEM(*parts_block),
                pltpu.SemaphoreType.DMA((POINTS // 128 + 2,)),
            ],
            name="tile",
            far_outs=(0, 2),
        ),
        2,
    )
    residual, first_image, send, keep = call(
        turn_kernel,
        [field, field, message, scalar_rows(3)],
        [got, right_side, image, parts, level_basis, coupling],
        8,
        1 << 28,
        scratch=[message_scratch, pltpu.SemaphoreType.DMA((1,))],
        name="turn",
        far_outs=(2,),
    )
    (image, _), got = tree(
        send,
        lambda: call(
            leaf_kernel,
            [field, scalar_rows(3)],
            [leaf_sizes, residual, first_image, tile, level_basis, coupling],
            8,
            1 << 30,
            scratch=[
                pltpu.VMEM((POINTS, POINTS), bf16),
                pltpu.SemaphoreType.DMA((HALVES,)),
            ],
            name="leaf",
            far_ins=(3,),
        ),
        3,
    )
    return tuple(
        call(
            end_kernel,
            [field, field],
            [got, right_side, residual, first_image, image, level_basis, coupling, keep],
            8,
            1 << 28,
            scratch=[
                pltpu.VMEM(*field),
                pltpu.VMEM(*field),
                pltpu.SemaphoreType.DMA((HALVES + 1,)),
            ],
            name="end",
            far_outs=(0, 1),
        )
    )


def solution(mesh):
    in_specs = (
        P(None, "pts"),
        P(None, "pts"),
        P("pts", None),
        P("pts", None),
        P(None, None, "pts"),
        P("pts", None, None, None),
    )
    out_specs = (P(None, "pts"), P(None, "pts"))
    return jax.shard_map(
        on_device, mesh=mesh, in_specs=in_specs, out_specs=out_specs, check_vma=False
    )
```

```python
import functools

import jax
import jax.numpy as jnp
from jax import lax
from jax.experimental import pallas as pl
from jax.experimental.pallas import tpu as pltpu
from jax.sharding import PartitionSpec as P

f32 = jnp.float32
bf16 = jnp.bfloat16

SQRT_THREE = 1.7320508075688772
NOISE_VAR = 1.0

RANK = 32
PROBES = 128
POINTS = 1024
PLANE = 32
DEPTH = 16
ROWS = 18
Z_ROWS = 8
LEAST = 384
MOST = 640
HALVES = 2

NT = (((1,), (1,)), ((), ()))
TN = (((0,), (0,)), ((), ()))
NN = (((1,), (0,)), ((), ()))


def first_row(level):
    if level < 5:
        return 2 * (level - 1)
    return 16 if level == 5 else 8 + 2 * (level - 6)


def dot(a, b, dims):
    return lax.dot_general(a, b, dims, preferred_element_type=f32)


def halves(x):
    high = x.astype(bf16)
    return high, (x - high.astype(f32)).astype(bf16)


def dot_split(a, b, dims):
    a_high, a_low = halves(a)
    b_high, b_low = halves(b)
    a_dim, b_dim = dims[0][0][0], dims[0][1][0]
    return dot(
        jnp.concatenate([a_high, a_high, a_low], axis=a_dim),
        jnp.concatenate([b_high, b_low, b_high], axis=b_dim),
        dims,
    )


def project_split(wide, v):
    high, low = halves(v)
    return dot(wide, high, NT) + dot(wide, low, NT)


def rows_of(products):
    part = products[:, :PROBES]
    for start in range(PROBES, POINTS, PROBES):
        part = part + products[:, start : start + PROBES]
    return jnp.sum(part.T, axis=0, keepdims=True)


def down_rows(row):
    square = jnp.broadcast_to(row, (PROBES, PROBES)).T
    return jnp.concatenate([square] * (POINTS // PROBES), axis=1)


def row_ids(rows):
    return lax.broadcasted_iota(jnp.int32, (rows, PROBES), 0)


def send_levels(projected, coupling_ref, send_ref):
    for level in range(1, 10):
        own = coupling_ref[0, level, :RANK, :]
        partial = dot_split(own, projected[RANK * (level - 1) : RANK * level], TN)
        for half in range(2):
            send_ref[pl.ds(first_row(level) + half, PLANE, stride=ROWS), :] = partial[
                PLANE * half : PLANE * (half + 1)
            ]


def start_kernel(
    right_hbm, basis_hbm, coupling_hbm, send_hbm,
    right_ref, basis_ref, coupling_ref, send_ref, sems,
):
    width = POINTS // HALVES
    fetches = []
    for half in range(HALVES):
        span = pl.ds(width * half, width)
        right_copy = pltpu.make_async_copy(
            right_hbm.at[:, span], right_ref.at[:, span], sems.at[2 * half]
        )
        basis_copy = pltpu.make_async_copy(
            basis_hbm.at[pl.ds(1, 9), :, span],
            basis_ref.at[:, :, span],
            sems.at[2 * half + 1],
        )
        right_copy.start()
        basis_copy.start()
        fetches.append((right_copy, basis_copy))
    used = (slice(None), pl.ds(1, 9), pl.ds(0, RANK))
    factors = pltpu.make_async_copy(
        coupling_hbm.at[used], coupling_ref.at[used], sems.at[2 * HALVES]
    )
    factors.start()
    projected = None
    for half, (right_copy, basis_copy) in enumerate(fetches):
        span = slice(width * half, width * (half + 1))
        right_copy.wait()
        basis_copy.wait()
        part = dot(
            basis_ref[:, :, span].reshape(9 * RANK, width),
            right_ref[:, span].astype(bf16),
            NT,
        )
        projected = part if half == 0 else projected + part
    factors.wait()
    send_levels(projected, coupling_ref, send_ref)
    out = pltpu.make_async_copy(send_ref, send_hbm, sems.at[2 * HALVES + 1])
    out.start()
    out.wait()


def leaf_level(v, rounded, leaf, boundary, basis_ref, coupling_ref):
    wide = basis_ref[0].astype(f32)
    in_first = lax.broadcasted_iota(jnp.int32, (RANK, POINTS), 1) < boundary
    both = jnp.concatenate(
        [jnp.where(in_first, wide, 0.0), jnp.where(in_first, 0.0, wide)], axis=0
    ).astype(bf16)
    factor = coupling_ref[0, 0]
    mixed = dot_split(factor, dot(both, rounded, NT), TN)
    coefficients = dot_split(factor, mixed, NN).astype(bf16)
    image = leaf + dot(coefficients, both, TN)
    curvature = rows_of(v * leaf) + jnp.sum(mixed * mixed, axis=0, keepdims=True)
    return image, curvature


def tile_kernel(
    coordinates_ref, order_ref, sizes_ref, right_ref, basis_ref, coupling_ref,
    tile_hbm, image_ref, parts_ref, scalars_ref,
    tile_ref, sems,
):
    boundary = sizes_ref[0, 0]
    order = order_ref[...]
    place, segment = jnp.bitwise_and(order, 127), jnp.right_shift(order, 7)
    sources = [
        jnp.concatenate(
            [coordinates_ref[:, start : start + 128], jnp.zeros((5, 128), f32)], axis=0
        )
        for start in range(0, POINTS, 128)
    ]
    pieces = []
    for start in range(0, POINTS, 128):
        lane = jnp.broadcast_to(place[:, start : start + 128], (8, 128))
        chosen = jnp.broadcast_to(segment[:, start : start + 128], (8, 128))
        piece = jnp.zeros((8, 128), f32)
        for number, source in enumerate(sources):
            piece = jnp.where(chosen == number, jnp.take_along_axis(source, lane, axis=1), piece)
        pieces.append(piece)
    x = jnp.concatenate(pieces, axis=1)
    x = SQRT_THREE * x
    column = x.T
    edge = boundary.astype(f32) - 0.5
    block = 128
    last = POINTS // block
    tile_ref[:LEAST, MOST:] = jnp.zeros((LEAST, POINTS - MOST), bf16)
    tile_ref[MOST:, :LEAST] = jnp.zeros((POINTS - MOST, LEAST), bf16)
    ids = lax.broadcasted_iota(jnp.int32, (block, block), 0)
    lanes = lax.broadcasted_iota(jnp.int32, (block, block), 1)
    diagonal = jnp.where(ids == lanes, NOISE_VAR, 0.0)
    row_side = ids.astype(f32) - edge
    col_side = lanes.astype(f32) - edge
    least, most = LEAST // block, MOST // block
    copies = []
    for up in range(last):
        rows = slice(block * up, block * (up + 1))
        down = [
            jnp.broadcast_to(column[rows, c : c + 1], (block, block)) for c in range(3)
        ]
        for across in range(up, most if up < least else last):
            columns = slice(block * across, block * (across + 1))
            dist_sq = None
            for c in range(3):
                offset = down[c] - x[c : c + 1, columns]
                dist_sq = offset * offset if c == 0 else dist_sq + offset * offset
            scaled = dist_sq * lax.rsqrt(jnp.maximum(dist_sq, 1e-37))
            values = (1.0 + scaled) * jnp.exp(-scaled)
            if across >= least and up < most:
                same = (row_side + block * up) * (col_side + block * across) > 0.0
                values = jnp.where(same, values, 0.0)
            if across == up:
                values = values + diagonal
            tile_ref[rows, columns] = values.astype(bf16)
            if across != up:
                tile_ref[columns, rows] = values.T.astype(bf16)
        span = pl.ds(block * up, block)
        copies.append(
            pltpu.make_async_copy(tile_ref.at[span], tile_hbm.at[span], sems.at[up])
        )
        copies[-1].start()

    v = right_ref[...]
    rounded = v.astype(bf16)
    leaf = dot(rounded, tile_ref[...], NN)
    image, curvature = leaf_level(v, rounded, leaf, boundary, basis_ref, coupling_ref)
    image_ref[...] = image
    scalars_ref[0:1, :] = curvature
    scalars_ref[1:2, :] = rows_of(v * v)
    wide = basis_ref[1:10].reshape(9 * RANK, POINTS)
    parts_ref[:, :PROBES] = project_split(wide, v)
    parts_ref[:, PROBES : 2 * PROBES] = project_split(wide, image)
    parts_ref[:, 2 * PROBES :] = dot(wide, wide, NT)
    for copy in copies:
        copy.wait()


def leaf_kernel(
    sizes_ref, residual_ref, first_image_ref, tile_hbm, basis_ref, coupling_ref,
    image_ref, scalars_ref, tile_ref, sems,
):
    width = POINTS // HALVES
    copies = []
    for half in range(HALVES):
        rows = pl.ds(width * half, width)
        copies.append(pltpu.make_async_copy(tile_hbm.at[rows], tile_ref.at[rows], sems.at[half]))
        copies[-1].start()
    v = residual_ref[...]
    rounded = v.astype(bf16)
    leaf = None
    for half in range(HALVES):
        span = slice(width * half, width * (half + 1))
        copies[half].wait()
        part = dot(rounded[:, span], tile_ref[span, :], NN)
        leaf = part if half == 0 else leaf + part
    image, curvature = leaf_level(
        v, rounded, leaf, sizes_ref[0, 0], basis_ref, coupling_ref
    )
    image_ref[...] = image
    scalars_ref[0:1, :] = curvature
    scalars_ref[1:2, :] = rows_of(v * v)
    scalars_ref[2:3, :] = rows_of(v * first_image_ref[...])


def pair_sums(got_ref):
    sums = [[got_ref[ROWS * d : ROWS * d + 8, :] for d in range(PLANE)]]
    for _ in range(4):
        last = sums[-1]
        sums.append([last[2 * i] + last[2 * i + 1] for i in range(len(last) // 2)])
    return sums


def total(got_ref, count, stride, start, rows):
    parts = [got_ref[stride * d + start : stride * d + start + rows, :] for d in range(count)]
    while len(parts) > 1:
        parts = [parts[2 * i] + parts[2 * i + 1] for i in range(len(parts) // 2)]
    return parts[0]


def squares(nodes):
    result = nodes[0] * nodes[0]
    for node in nodes[1:]:
        result = result + node * node
    return result


def plane_kernel(count, got_ref, scalars_ref, send_ref):
    ids = row_ids(8)
    sums = pair_sums(got_ref)
    square = jnp.zeros((8, PROBES), f32)
    for level in range(1, 5):
        square = jnp.where(ids // 2 == level - 1, squares(sums[level]), square)
    fifth = total(got_ref, PLANE, ROWS, 16, 2)
    curvature = jnp.sum(square, axis=0, keepdims=True) + jnp.sum(
        fifth * fifth, axis=0, keepdims=True
    )
    scalars = scalars_ref[...] + jnp.where(row_ids(count) == 0, curvature, 0.0)
    block = jnp.concatenate([total(got_ref, PLANE, ROWS, 8, 8), scalars], axis=0)
    stride = Z_ROWS + count
    for z in range(DEPTH):
        send_ref[stride * z : stride * (z + 1), :] = block


def depth_kernel(count, got_ref, z_got_ref, send_ref):
    z_stride, stride = Z_ROWS + count, ROWS + count
    own = lax.axis_index("pts") // PLANE
    ids = row_ids(8)
    reach = jnp.left_shift(2, ids // 2)
    pair = jnp.zeros((8, PROBES), f32)
    nodes = []
    for z in range(DEPTH):
        block = z_got_ref[z_stride * z : z_stride * z + 8, :]
        nodes.append(block)
        apart = jnp.bitwise_xor(own, z)
        pair = pair + jnp.where(apart < reach, block, 0.0)
    square = jnp.zeros((8, PROBES), f32)
    for level in range(4):
        nodes = [nodes[2 * i] + nodes[2 * i + 1] for i in range(len(nodes) // 2)]
        square = jnp.where(ids // 2 == level, squares(nodes), square)
    curvature = jnp.sum(square, axis=0, keepdims=True)
    scalars = total(z_got_ref, DEPTH, z_stride, 8, count)
    scalars = scalars + jnp.where(row_ids(count) == 0, curvature, 0.0)
    tail = jnp.concatenate([pair, total(got_ref, PLANE, ROWS, 16, 2), scalars], axis=0)
    sums = pair_sums(got_ref)
    for d in range(PLANE):
        first = sums[4][d >> 4]
        for level in (3, 2, 1):
            first = jnp.where(ids // 2 == level - 1, sums[level][d >> level], first)
        send_ref[stride * d : stride * d + 8, :] = first
        send_ref[stride * d + 8 : stride * (d + 1), :] = tail


def level_coefficients(got_ref, coupling_ref, stride):
    coefficients = []
    for level in range(1, 10):
        mixed = jnp.concatenate(
            [
                got_ref[pl.ds(first_row(level) + half, PLANE, stride=stride), :]
                for half in range(2)
            ],
            axis=0,
        )
        coefficients.append(dot_split(coupling_ref[0, level, :RANK, :], mixed, NN))
    return jnp.concatenate(coefficients, axis=0).astype(bf16)


def expand(coefficients, basis_ref, span):
    width = span.stop - span.start
    return dot(coefficients, basis_ref[1:10, :, span].reshape(9 * RANK, width), TN)


def turn_kernel(
    got_ref, right_ref, image_ref, parts_ref, basis_ref, coupling_ref,
    residual_ref, whole_image_ref, send_hbm, keep_ref, send_ref, sem,
):
    scalars = total(got_ref, PLANE, ROWS + 2, ROWS, 2)
    curvature, norm = scalars[0:1], scalars[1:2]
    step = norm / curvature
    coefficients = level_coefficients(got_ref, coupling_ref, ROWS + 2)
    gram_high, gram_low = halves(parts_ref[:, 2 * PROBES :])
    spread = dot(gram_high, coefficients, NN) + dot(gram_low, coefficients, NN)
    projected = parts_ref[:, :PROBES] - step * (parts_ref[:, PROBES : 2 * PROBES] + spread)
    send_levels(projected, coupling_ref, send_ref)
    out = pltpu.make_async_copy(send_ref, send_hbm, sem.at[0])
    out.start()
    whole = image_ref[...] + expand(coefficients, basis_ref, slice(0, POINTS))
    whole_image_ref[...] = whole
    residual_ref[...] = right_ref[...] - down_rows(step) * whole
    keep_ref[0:1, :] = step
    keep_ref[1:2, :] = curvature
    keep_ref[2:3, :] = norm
    out.wait()


def end_kernel(
    got_ref, right_ref, residual_ref, first_image_ref, image_ref, basis_ref, coupling_ref,
    keep_ref, solution_hbm, last_hbm, solution_ref, last_ref, sems,
):
    scalars = total(got_ref, PLANE, ROWS + 3, ROWS, 3)
    own, norm, cross = scalars[0:1], scalars[1:2], scalars[2:3]
    step, curvature, norm_before = keep_ref[0:1, :], keep_ref[1:2, :], keep_ref[2:3, :]
    ratio = norm / norm_before
    step_now = norm / (own + 2.0 * ratio * cross + ratio * ratio * curvature)
    ratio_down, step_down = down_rows(ratio), down_rows(step_now)
    right, residual = right_ref[...], residual_ref[...]
    direction = residual + ratio_down * right
    solution_ref[...] = down_rows(step) * right + step_down * direction
    copies = [pltpu.make_async_copy(solution_ref, solution_hbm, sems.at[HALVES])]
    copies[0].start()
    coefficients = level_coefficients(got_ref, coupling_ref, ROWS + 3)
    width = POINTS // HALVES
    for half in range(HALVES):
        span = slice(width * half, width * (half + 1))
        image = image_ref[:, span] + expand(coefficients, basis_ref, span)
        image = image + ratio_down[:, span] * first_image_ref[:, span]
        last_ref[:, span] = residual[:, span] - step_down[:, span] * image
        columns = pl.ds(width * half, width)
        copies.append(
            pltpu.make_async_copy(
                last_ref.at[:, columns], last_hbm.at[:, columns], sems.at[half]
            )
        )
        copies[-1].start()
    for copy in copies:
        copy.wait()


VMEM = pl.BlockSpec(memory_space=pltpu.VMEM)
SMEM = pl.BlockSpec(memory_space=pltpu.SMEM)
HBM = pl.BlockSpec(memory_space=pltpu.HBM)


def call(body, outs, ins, megabytes, cost, scratch=(), name=None, far_ins=(), far_outs=()):
    specs = [SMEM if a.dtype == jnp.int32 and a.shape == (1, 2) else VMEM for a in ins]
    for place in far_ins:
        specs[place] = HBM
    return pl.pallas_call(
        body,
        out_shape=[
            (pltpu.HBM if place in far_outs else jax.ShapeDtypeStruct)(shape, kind)
            for place, (shape, kind) in enumerate(outs)
        ],
        in_specs=specs,
        out_specs=[HBM if place in far_outs else VMEM for place in range(len(outs))],
        scratch_shapes=list(scratch),
        compiler_params=pltpu.CompilerParams(vmem_limit_bytes=megabytes << 20),
        cost_estimate=pl.CostEstimate(flops=cost, bytes_accessed=2 << 20, transcendentals=0),
        name=name,
    )(*ins)


def plane_groups(count):
    return [list(range(PLANE * z, PLANE * (z + 1))) for z in range(count // PLANE)]


def depth_groups(count):
    return [list(range(place, count, PLANE)) for place in range(PLANE)]


def exchange(rows, groups):
    members = len(groups[0])
    blocks = rows.reshape(members, 1, rows.shape[0] // members * PROBES)
    got = lax.all_to_all(blocks, "pts", 0, 0, axis_index_groups=groups)
    return got.reshape(rows.shape)


def on_device(right_side, coordinates, tree_order, leaf_sizes, level_basis, coupling):
    count = lax.axis_size("pts")
    planes, depths = plane_groups(count), depth_groups(count)
    field = ((PROBES, POINTS), f32)
    message = ((PLANE * ROWS, PROBES), f32)
    message_scratch = pltpu.VMEM(*message)
    parts_block = ((9 * RANK, 2 * PROBES + 9 * RANK), f32)

    def scalar_rows(rows):
        return ((rows, PROBES), f32)

    def tree(send, scalars_of, rows):
        got = exchange(send, planes)
        local = scalars_of()
        (z_send,) = call(
            functools.partial(plane_kernel, rows),
            [((DEPTH * (Z_ROWS + rows), PROBES), f32)],
            [got, local[-1]],
            2,
            1 << 20,
            name="plane",
        )
        z_got = exchange(z_send, depths)
        (back,) = call(
            functools.partial(depth_kernel, rows),
            [((PLANE * (ROWS + rows), PROBES), f32)],
            [got, z_got],
            2,
            1 << 20,
            name="depth",
        )
        return local, exchange(back, planes)

    (send,) = call(
        start_kernel,
        [message],
        [right_side, level_basis, coupling],
        60,
        1 << 26,
        scratch=[
            pltpu.VMEM(right_side.shape, f32),
            pltpu.VMEM((9, RANK, POINTS), bf16),
            pltpu.VMEM(coupling.shape, f32),
            message_scratch,
            pltpu.SemaphoreType.DMA((2 * HALVES + 2,)),
        ],
        name="start",
        far_ins=(0, 1, 2),
        far_outs=(0,),
    )
    (tile, image, parts, _), got = tree(
        send,
        lambda: call(
            tile_kernel,
            [((POINTS, POINTS), bf16), field, parts_block, scalar_rows(2)],
            [coordinates, tree_order, leaf_sizes, right_side, level_basis, coupling],
            12,
            4 << 30,
            scratch=[
                pltpu.VMEM((POINTS, POINTS), bf16),
                pltpu.SemaphoreType.DMA((POINTS // 128,)),
            ],
            name="tile",
            far_outs=(0,),
        ),
        2,
    )
    residual, first_image, send, keep = call(
        turn_kernel,
        [field, field, message, scalar_rows(3)],
        [got, right_side, image, parts, level_basis, coupling],
        8,
        1 << 28,
        scratch=[message_scratch, pltpu.SemaphoreType.DMA((1,))],
        name="turn",
        far_outs=(2,),
    )
    (image, _), got = tree(
        send,
        lambda: call(
            leaf_kernel,
            [field, scalar_rows(3)],
            [leaf_sizes, residual, first_image, tile, level_basis, coupling],
            8,
            1 << 30,
            scratch=[
                pltpu.VMEM((POINTS, POINTS), bf16),
                pltpu.SemaphoreType.DMA((HALVES,)),
            ],
            name="leaf",
            far_ins=(3,),
        ),
        3,
    )
    return tuple(
        call(
            end_kernel,
            [field, field],
            [got, right_side, residual, first_image, image, level_basis, coupling, keep],
            8,
            1 << 28,
            scratch=[
                pltpu.VMEM(*field),
                pltpu.VMEM(*field),
                pltpu.SemaphoreType.DMA((HALVES + 1,)),
            ],
            name="end",
            far_outs=(0, 1),
        )
    )


def solution(mesh):
    in_specs = (
        P(None, "pts"),
        P(None, "pts"),
        P("pts", None),
        P("pts", None),
        P(None, None, "pts"),
        P("pts", None, None, None),
    )
    out_specs = (P(None, "pts"), P(None, "pts"))
    return jax.shard_map(
        on_device, mesh=mesh, in_specs=in_specs, out_specs=out_specs, check_vma=False
    )
```
